256 devices in a mesh: dom: 64 (over y, z_hi, x, core), sub: 4 (over z_lo).
Axes of the slice: x: 4, y: 4, z: 8 (z_hi: 2, z_lo: 4; z = z_hi * 4 + z_lo), core: 2. Of those that a mesh axis runs over, the one named last changes fastest.
Arguments:
- nodes: bfloat16 [524288, 128], P(('dom', 'sub')), may hold values from -6 to 6
- weights: bfloat16 [4, 6, 128, 128], replicated, may hold values from -0.5 to 0.5
- edge_src: int32 [256, 12288], P(('dom', 'sub')), may hold values from 0 to 2303, as said below
- edge_dst: int32 [256, 12288], P(('dom', 'sub')), may hold values from 0 to 2047, as said below
- edge_valid: int32 [256, 12288], P(('dom', 'sub')), may hold values 0 or 1
- ghost_list: int32 [256, 2, 128], P(('dom', 'sub')), may hold values from 0 to 2047
- cluster_of: int32 [256, 2048], P(('dom', 'sub')), may hold values from 0 to 127
- owner: int32 [256, 128, 1], P(('dom', 'sub')), may hold values from 0 to 63; in each aligned block of 128 rows (0 to 127, 128 to 255, ..., all dimensions but the last counted through in order) at most 4 rows name the same one
- coarse_row: int32 [256, 128], P(('dom', 'sub')), may hold values from 0 to 127
- coarse_src: int32 [64, 768], P('dom'), may hold values from 0 to 159
- coarse_dst: int32 [64, 768], P('dom'), may hold values from 0 to 127
- coarse_ghosts: int32 [64, 2, 16], P('dom'), may hold values from 0 to 127
Outputs:
- fine_out: bfloat16 [524288, 128], P(('dom', 'sub'))
- coarse_out: bfloat16 [8192, 128], P('dom')
The draws below stay inside these ranges and needn't reach their ends.
Inputs may be any that keep to these rules, and one draw needn't show every extreme that they name: Among the 128 clusters of any one device at most 4 have the same owner, and some owner has exactly 4 of them. `edge_dst`: A device's edge slots come in blocks of 768 slots; the slots of block b have destinations among rows b * 128 to b * 128 + 127. `edge_src`: read the device's table as the line of its lower neighbour's ghost rows, then its own 2048 rows, then its upper neighbour's ghost rows; the slots of edge block b have sources among positions b * 128 to b * 128 + 3 * 128 - 1 of that line.
All inputs are finite; a program needn't handle non-finite values. No bound on the sum of `edge_valid` on one device may be relied on, other than what follows from the above.
Results may differ from the reference program's by a relative error of at most 0.022.
Values may be sent and summed in bfloat16 or wider, within the bound.
No kernel may reach another device: no remote copies, remote signals or barrier semaphores. Data moves between devices by JAX's collectives and lax.ppermute only.
A program may use at most 64 MiB of HBM per device.

```python
import math
import jax
import jax.numpy as jnp
import numpy as np
from jax import lax

H = 128
NF = 2048
LC = 128
LAYERS = 4
EF = 12288
GH = 128
CAP = 4
NCD = 128
EC = 768
CGH = 16
NFT = 524288
NCT = 8192
N_DOM = 64
DEVICES = 256


def draw_edge_dst(key, part):
    key = jax.random.fold_in(key, 11)
    offsets = jax.random.randint(key, (DEVICES, EF), 0, GH, dtype=jnp.int32)
    block_of = (jnp.arange(EF, dtype=jnp.int32) // (6 * GH))[None, :]
    return (block_of * GH + offsets).astype(jnp.int32)


def draw_edge_src(key, part):
    key = jax.random.fold_in(key, 12)
    offsets = jax.random.randint(key, (DEVICES, EF), 0, 3 * GH, dtype=jnp.int32)
    block_of = (jnp.arange(EF, dtype=jnp.int32) // (6 * GH))[None, :]
    line = block_of * GH + offsets
    table = jnp.where(line < GH, NF + line, jnp.where(line < GH + NF, line - GH, line))
    return table.astype(jnp.int32)


def touch_ends(result, stream_key, least, largest):
    place = [jax.random.randint(jax.random.fold_in(stream_key, axis), (), 0, length) for axis, length in enumerate(result.shape)]
    main_axis = result.shape.index(max(result.shape))
    neighbour = place[:main_axis] + [(place[main_axis] + 1) % result.shape[main_axis]] + place[main_axis + 1:]
    return result.at[tuple(place)].set(least).at[tuple(neighbour)].set(largest)


def shard_levels(own_key, extent, split, smallest, largest):
    def one(axis_at, shards_of):
        steps = jax.random.uniform(jax.random.fold_in(jax.random.fold_in(own_key, 6), axis_at), (shards_of,), jnp.float32, smallest / len(split), largest / len(split))
        return jnp.repeat(jnp.exp(steps), extent[axis_at] // shards_of).reshape((-1,) + (1,) * (len(extent) - axis_at - 1))

    gain = one(*split[0])
    for cut in split[1:]:
        gain = gain * one(*cut)
    return gain


def assign_block(stream_key, own, number, rows, count, top, most, lean):
    ranking = jax.random.permutation(stream_key, count)
    packed, usual = shares(count, rows * top, most, lean, True), shares(count, rows * top, most, lean, False)
    places = jnp.arange(count)

    def named(sizes, offset_by):
        used = int((sizes > 0).sum())
        fixed = max(1, used // 4)
        shifted = fixed + (places - fixed + offset_by * (used - fixed)) % max(1, count - fixed)
        return jnp.zeros((count,), jnp.int32).at[ranking[jnp.where(places < fixed, places, shifted)]].set(jnp.asarray(sizes, jnp.int32))

    sizes = jnp.where(number % 4 == 0, named(packed, number // 4), named(usual, number - number // 4 - 1))
    mixed = jax.random.permutation(jax.random.fold_in(own, 3), count)
    donor, receiver = mixed[0:count // 2 * 2:2], mixed[1:count // 2 * 2:2]
    room = jnp.minimum(sizes[donor] - 1, most - sizes[receiver]) // 2
    room = jnp.where((donor == ranking[0]) | (receiver == ranking[0]) | (sizes[receiver] == 0), 0, jnp.maximum(room, 0))
    shifted = jax.random.randint(jax.random.fold_in(own, 4), (count // 2,), 0, 1 << 20) % (room + 1)
    sizes = sizes.at[donor].add(-shifted).at[receiver].add(shifted)
    items = jnp.searchsorted(jnp.cumsum(sizes), jnp.arange(rows * top), side="right").astype(jnp.int32)
    table = items.reshape(top, rows).T
    table = table[jax.random.permutation(jax.random.fold_in(own, 1), rows)]
    offset_by = jax.random.randint(jax.random.fold_in(own, 2), (rows, 1), 0, top)
    return jnp.take_along_axis(table, (jnp.arange(top)[None, :] + offset_by) % top, axis=1)


def shares(amount, total, limit, lean, full):
    weights = [(1 << 20) // math.isqrt(grade ** lean) + 1 for grade in range(1, amount + 1)]
    largest = limit if full else min(limit, max(-(-total // amount), total * weights[0] // sum(weights)))
    least = 1 if total - largest >= amount - 1 else 0
    holding, rest = [largest] + [least] * (amount - 1), total - largest - least * (amount - 1)
    while rest > 0:
        movable = [i for i in range(1, amount) if holding[i] < largest] or [i for i in range(1, amount) if holding[i] < limit]
        whole, left = sum([weights[i] for i in movable]), rest
        for i in movable:
            extra = min(limit - holding[i], max(1, left * weights[i] // whole), rest)
            holding[i] = holding[i] + extra
            rest = rest - extra
    return np.array(holding)


def noise(key, shape, width, limit, split=(), kind=jnp.bfloat16):
    loudness = shard_levels(key, shape, split, -0.22, 0.18) if split else 1.0
    entries = jax.random.normal(key, shape, jnp.float32) * width * loudness
    return jnp.minimum(jnp.maximum(entries, -limit), limit).astype(kind)


def setup_inputs(seed: int = 0) -> dict:
    streams_of = jax.random.split(jax.random.key(seed), 13)
    nodes = noise(streams_of[0], (NFT, H), 1.0, 6.0, ((0, 256),))
    weights = noise(streams_of[1], (LAYERS, 6, H, H), H ** -0.5, 0.5)
    edge_src = draw_edge_src(jax.random.fold_in(streams_of[12], 71), 0)
    edge_dst = draw_edge_dst(jax.random.fold_in(streams_of[12], 71), 0)
    edge_valid = touch_ends((jax.random.randint(streams_of[4], (DEVICES, EF), 0, 8) < 7).astype(jnp.int32), jax.random.fold_in(streams_of[4], 1), 0, 1)
    ghost_list = touch_ends(jax.random.randint(streams_of[5], (DEVICES, 2, GH), 0, NF), jax.random.fold_in(streams_of[5], 1), 0, NF - 1).astype(jnp.int32)
    cluster_of = touch_ends(jax.random.randint(streams_of[6], (DEVICES, NF), 0, LC), jax.random.fold_in(streams_of[6], 1), 0, LC - 1).astype(jnp.int32)
    owner_keys = jax.random.split(jax.random.fold_in(streams_of[7], 1), DEVICES * LC // LC)
    owner_turns = jax.random.permutation(jax.random.fold_in(streams_of[7], 3), DEVICES * LC // LC)
    owner = jax.vmap(lambda own, number: assign_block(jax.random.fold_in(streams_of[7], 2), own, number, LC, N_DOM, 1, CAP, 2))(owner_keys, owner_turns).reshape((DEVICES, LC, 1))
    coarse_row = touch_ends(jax.random.randint(streams_of[8], (DEVICES, LC), 0, NCD), jax.random.fold_in(streams_of[8], 1), 0, NCD - 1).astype(jnp.int32)
    coarse_src = touch_ends(jax.random.randint(streams_of[9], (N_DOM, EC), 0, NCD + 2 * CGH), jax.random.fold_in(streams_of[9], 1), 0, (NCD + 2 * CGH) - 1).astype(jnp.int32)
    coarse_dst = touch_ends(jax.random.randint(streams_of[10], (N_DOM, EC), 0, NCD), jax.random.fold_in(streams_of[10], 1), 0, NCD - 1).astype(jnp.int32)
    coarse_ghosts = touch_ends(jax.random.randint(streams_of[11], (N_DOM, 2, CGH), 0, NCD), jax.random.fold_in(streams_of[11], 1), 0, NCD - 1).astype(jnp.int32)
    return dict(nodes=nodes, weights=weights, edge_src=edge_src, edge_dst=edge_dst, edge_valid=edge_valid, ghost_list=ghost_list, cluster_of=cluster_of, owner=owner, coarse_row=coarse_row, coarse_src=coarse_src, coarse_dst=coarse_dst, coarse_ghosts=coarse_ghosts)


def layer_norm(values):
    average = lax.optimization_barrier(jnp.mean(values, axis=-1, keepdims=True))
    centred = values - average
    spread = lax.optimization_barrier(jnp.mean(centred * centred, axis=-1, keepdims=True))
    return centred * lax.rsqrt(spread + 1e-05)

def local_layer(block_rows, from_left, from_right, edge_from, edge_to, valid, layer_weights):
    lookup = jnp.concatenate([block_rows, from_left, from_right], axis=0)
    source = jnp.dot(lookup, layer_weights[0], preferred_element_type=jnp.float32).astype(jnp.bfloat16)
    target = jnp.dot(block_rows, layer_weights[1], preferred_element_type=jnp.float32).astype(jnp.bfloat16)
    summed = source[edge_from].astype(jnp.float32) + target[edge_to].astype(jnp.float32)
    activated = jax.nn.silu(summed).astype(jnp.bfloat16)
    message = jnp.dot(activated, layer_weights[2], preferred_element_type=jnp.float32)
    message = (message * valid[:, None].astype(jnp.float32)).astype(jnp.bfloat16)
    gathered = jax.ops.segment_sum(message.astype(jnp.float32), edge_to, num_segments=block_rows.shape[0])
    gathered = gathered.astype(jnp.bfloat16)
    hidden = jnp.dot(block_rows, layer_weights[3], preferred_element_type=jnp.float32)
    hidden = hidden + jnp.dot(gathered, layer_weights[4], preferred_element_type=jnp.float32)
    hidden = jax.nn.silu(hidden).astype(jnp.bfloat16)
    update = jnp.dot(hidden, layer_weights[5], preferred_element_type=jnp.float32)
    return (block_rows.astype(jnp.float32) + layer_norm(update)).astype(jnp.bfloat16)

def level_layer(states, lists, edge_from, edge_to, valid, layer_weights):
    to_lower = jax.vmap(lambda rows_of, indices: rows_of[indices])(states, lists[:, 0])
    to_upper = jax.vmap(lambda rows_of, indices: rows_of[indices])(states, lists[:, 1])
    nothing = jnp.zeros_like(to_lower[:1])
    from_left = jnp.concatenate([nothing, to_upper[:-1]], axis=0)
    from_right = jnp.concatenate([to_lower[1:], nothing], axis=0)

    def apply_one(pieces):
        return local_layer(pieces[0], pieces[1], pieces[2], pieces[3], pieces[4], pieces[5], layer_weights)
    return lax.map(apply_one, (states, from_left, from_right, edge_from, edge_to, valid))

def reference(nodes, weights, edge_src, edge_dst, edge_valid, ghost_list, cluster_of, owner, coarse_row, coarse_src, coarse_dst, coarse_ghosts):
    blocks = edge_src.shape[0]
    states = nodes.reshape(blocks, NF, H)
    for layer_id in range(2):
        states = level_layer(states, ghost_list, edge_src, edge_dst, edge_valid, weights[layer_id])
    cluster_target = owner[:, :, 0] * NCD + coarse_row
    fine_target = jnp.take_along_axis(cluster_target, cluster_of, axis=1).reshape(-1)
    flattened = states.reshape(-1, H)
    pooled_sums = jax.ops.segment_sum(flattened.astype(jnp.float32), fine_target, num_segments=NCT)
    counts = jax.ops.segment_sum(jnp.ones(fine_target.shape, jnp.float32), fine_target, num_segments=NCT)
    coarse = (pooled_sums / jnp.maximum(counts, 1.0)[:, None]).astype(jnp.bfloat16)
    all_valid = jnp.ones(coarse_src.shape, jnp.int32)
    coarse = level_layer(coarse.reshape(N_DOM, NCD, H), coarse_ghosts, coarse_src, coarse_dst, all_valid, weights[2])
    coarse = coarse.reshape(NCT, H)
    lifted = (flattened.astype(jnp.float32) + coarse[fine_target].astype(jnp.float32)).astype(jnp.bfloat16)
    states = level_layer(lifted.reshape(blocks, NF, H), ghost_list, edge_src, edge_dst, edge_valid, weights[3])
    return (states.reshape(-1, H), coarse)
```

```python
import functools

import jax
import jax.numpy as jnp
from jax import lax
from jax.experimental import pallas as pl
from jax.experimental.pallas import tpu as pltpu
from jax.sharding import PartitionSpec as P

BF = jnp.bfloat16
F32 = jnp.float32
I32 = jnp.int32
I16 = jnp.int16
NN = (((1,), (0,)), ((), ()))
NT = (((1,), (1,)), ((), ()))
TN = (((0,), (0,)), ((), ()))

GH = 128
CAP = 4
SLOTS = 16
VMEM_LIMIT = 28 << 20


def dot(left, right, dims=NN):
    return lax.dot_general(left, right, dims, preferred_element_type=F32)


def iota(shape, dim, dtype=I32):
    return lax.broadcasted_iota(I32, shape, dim).astype(dtype)


def hot(mask):
    return jnp.where(mask, 1.0, 0.0).astype(BF)


def column(row):
    return jnp.broadcast_to(row.astype(F32), (128, 128)).T


def half_silu(half):
    return half * (1.0 + jnp.tanh(half))


def rows_hot(index_row, count):
    table = lax.broadcasted_iota(I16, (count, index_row.shape[1]), 0)
    return jnp.where(table == index_row.astype(I16), BF(1), BF(0))


def edge_sum(source_t, target_t, from_row, to_row):
    from_hot = rows_hot(from_row, source_t.shape[1])
    to_hot = rows_hot(to_row, target_t.shape[1])
    table = jnp.concatenate([source_t, target_t], axis=1)
    half = dot(table, jnp.concatenate([from_hot, to_hot], axis=0))
    return dot(to_hot, half_silu(half).astype(BF), NT).astype(BF)


def node_weights(w):
    both = jnp.concatenate([w[3] * BF(0.5), (dot(w[2], w[4]) * 0.5).astype(BF)], axis=0)
    last = w[5].astype(F32)
    return both, (last - jnp.mean(last, axis=1, keepdims=True)).astype(BF)


def node_update(rows, sums, both, last):
    half = dot(jnp.concatenate([rows, sums], axis=1), both)
    centred = dot(half_silu(half).astype(BF), last)
    spread = jnp.mean(centred * centred, axis=1, keepdims=True)
    return (rows.astype(F32) + centred * lax.rsqrt(spread + 1e-5)).astype(BF)


def local_edges(b, row_count, src, dst, valid, width):
    at = pl.ds(b * width, width)
    edge = src[:, at]
    line = jnp.where(
        edge < row_count, edge + GH, jnp.where(edge < row_count + GH, edge - row_count, edge)
    )
    return line - b * GH, jnp.where(valid[:, at] != 0, dst[:, at] - b * GH, -1)


def pick_rows(rows_ref, list_row):
    count = rows_ref.shape[0]
    wanted = column(list_row)
    lanes = iota((128, 128), 1, F32)
    table = jnp.concatenate(
        [hot(wanted == lanes + float(128 * k)) for k in range(count // 128)], axis=1
    )
    return dot(table, rows_ref[...]).astype(BF)


def pick_both(rows_ref, lists, odd, near, far):
    to_lower, to_upper = lists[0:1, :], lists[1:2, :]
    near[...] = pick_rows(rows_ref, jnp.where(odd, to_lower, to_upper))
    far[...] = pick_rows(rows_ref, jnp.where(odd, to_upper, to_lower))


def pick_kernel(place, rows_ref, lists, near, far):
    pick_both(rows_ref, lists, place[1] % 2 == 1, near, far)


def inner_kernel(layer, rows_ref, weights, src, dst, valid, out, source, target, sums):
    w = [weights[layer, i] for i in range(6)]
    row_count = rows_ref.shape[0]
    blocks = row_count // GH
    width = src.shape[1] // blocks
    source[...] = dot(w[0] * BF(0.5), rows_ref[...], (((0,), (1,)), ((), ()))).astype(BF)
    target[...] = dot(w[1] * BF(0.5), rows_ref[...], (((0,), (1,)), ((), ()))).astype(BF)
    for b in range(1, blocks - 1):
        from_row, to_row = local_edges(b, row_count, src, dst, valid, width)
        sums[b * GH : (b + 1) * GH, :] = edge_sum(
            source[:, (b - 1) * GH : (b + 2) * GH],
            target[:, b * GH : (b + 1) * GH],
            from_row,
            to_row,
        )
    both, last = node_weights(w)
    step = 2 * GH
    for first in range(GH, row_count - GH, step):
        at = pl.ds(first, step)
        out[at, :] = node_update(rows_ref[at, :], sums[at, :], both, last)


def end_rows(layer, place, rows_ref, inner, from_near, from_far, weights, src, dst, valid, out):
    w = [weights[layer, i] for i in range(6)]
    odd = place[1] % 2 == 1
    row_count = rows_ref.shape[0]
    blocks = row_count // GH
    width = src.shape[1] // blocks
    near, far = from_near[...], from_far[...]
    before = jnp.where(odd, near, far)
    after = jnp.where(odd, far, near)
    ends = [
        (0, before, rows_ref[0 : 2 * GH, :], rows_ref[0:GH, :]),
        (
            blocks - 1,
            rows_ref[row_count - 2 * GH :, :],
            after,
            rows_ref[row_count - GH :, :],
        ),
    ]
    out[GH : row_count - GH, :] = inner[GH : row_count - GH, :]
    sums, own = [], []
    for b, lower, upper, rows in ends:
        line = jnp.concatenate([lower, upper], axis=0)
        source = dot(w[0] * BF(0.5), line, (((0,), (1,)), ((), ()))).astype(BF)
        target = dot(w[1] * BF(0.5), rows, (((0,), (1,)), ((), ()))).astype(BF)
        from_row, to_row = local_edges(b, row_count, src, dst, valid, width)
        sums.append(edge_sum(source, target, from_row, to_row))
        own.append(rows)
    both, last = node_weights(w)
    new = node_update(
        jnp.concatenate(own, axis=0), jnp.concatenate(sums, axis=0), both, last
    )
    out[0:GH, :] = new[:GH]
    out[row_count - GH :, :] = new[GH:]


def ends_kernel(layer, place, rows_ref, inner, from_near, from_far, weights, src, dst, valid, out):
    end_rows(layer, place, rows_ref, inner, from_near, from_far, weights, src, dst, valid, out)


def ends_pick_kernel(
    layer, place, rows_ref, inner, from_near, from_far, weights, src, dst, valid, lists, out, near, far
):
    end_rows(layer, place, rows_ref, inner, from_near, from_far, weights, src, dst, valid, out)
    pick_both(out, lists, place[1] % 2 == 1, near, far)


def ends_pool_kernel(
    layer,
    place,
    rows_ref,
    inner,
    from_near,
    from_far,
    weights,
    src,
    dst,
    valid,
    cluster,
    slot_pick,
    facts,
    out,
    parcel,
):
    end_rows(layer, place, rows_ref, inner, from_near, from_far, weights, src, dst, valid, out)
    member = rows_hot(cluster[...], 128)
    partial = dot(member, out[...]).astype(BF)
    parcel[...] = dot(slot_pick[...], jnp.concatenate([partial, facts[...]], axis=0)).astype(BF)


def prepare_kernel(cluster, owner, coarse_row, ghosts, slot_pick, facts, slot_of):
    member = rows_hot(cluster[...], 128)
    counts = jnp.sum(member.astype(F32), axis=1, keepdims=True)
    owner_row = owner[...].astype(F32)
    by_row, by_lane = column(owner_row), jnp.broadcast_to(owner_row, (128, 128))
    sub, lane = iota((128, 128), 0), iota((128, 128), 1)
    same = by_row == by_lane
    place_col = jnp.sum(jnp.where(same & (lane < sub), 1.0, 0.0), axis=1, keepdims=True)
    place_row = jnp.sum(jnp.where(same & (sub < lane), 1.0, 0.0), axis=0, keepdims=True)
    slot_row = owner_row * CAP + place_row
    slot_col = by_row * CAP + place_col
    owners = slot_pick.shape[0] // SLOTS
    slot_of[...] = hot(
        jnp.concatenate([slot_col] * (CAP * owners // 128), axis=1)
        == iota((128, CAP * owners), 1, F32)
    )
    row = iota((owners * SLOTS, 128), 0)
    to, at = row // SLOTS, row % SLOTS
    label = jnp.where(
        at < CAP,
        CAP * to + at,
        jnp.where(
            at < 2 * CAP,
            CAP * (to - 1) + at - CAP,
            jnp.where(at < 3 * CAP, CAP * (to + 1) + at - 2 * CAP, -1),
        ),
    )
    slot_pick[:, 0:128] = hot(label.astype(F32) == slot_row)
    fact = jnp.where(
        at == 3 * CAP,
        to,
        jnp.where(
            at == 3 * CAP + 1,
            to - 1,
            jnp.where(at == 3 * CAP + 2, to + 1, jnp.where(at == 3 * CAP + 3, 127, -1)),
        ),
    )
    slot_pick[:, 128:256] = hot(fact == iota(fact.shape, 1))
    high = jnp.floor(counts / 16.0)
    low = counts - 16.0 * high
    lanes = lane.astype(F32)
    values = (
        jnp.where(lanes == place_col, column(coarse_row[...]), 0.0)
        + jnp.where(lanes == place_col + CAP, high, 0.0)
        + jnp.where(lanes == place_col + 2 * CAP, low, 0.0)
    ).astype(BF)
    meta = dot(hot(by_lane == sub.astype(F32)), values)
    listed = jnp.concatenate(
        [ghosts[...].astype(F32), jnp.zeros((1, 128 - ghosts.shape[1]), F32)], axis=1
    )
    facts[...] = jnp.where(sub == 127, listed, meta).astype(BF)


def received_kernel(place, got, part, back):
    total = got.shape[0]
    owners = total // SLOTS
    here = place[0]
    wide = iota((3 * owners, total), 1)
    pick = iota((3 * owners, total), 0)
    metas = dot(
        hot(wide == SLOTS * (pick % owners) + 3 * CAP + pick // owners), got[...]
    ).astype(BF)
    spread = hot((wide // SLOTS == pick % owners) & (wide % SLOTS // CAP == pick // owners))
    facts = dot(metas, spread, TN)[0:16]
    lane = iota((1, total), 1)
    turn = iota((16, total), 0) - iota((16, total), 1) % CAP

    def fact(number):
        return jnp.sum(jnp.where(turn == CAP * number, facts, 0.0), axis=0, keepdims=True)

    group = lane % SLOTS // CAP
    key = jnp.where(group < 3, fact(0) + (128 * group).astype(F32), -1.0)
    below = got[pl.ds(pl.multiple_of(jnp.maximum(here - 1, 0) * SLOTS, SLOTS), SLOTS), :]
    above = got[pl.ds(pl.multiple_of(jnp.minimum(here + 1, owners - 1) * SLOTS, SLOTS), SLOTS), :]
    below = column(below.astype(F32)[SLOTS - 1 : SLOTS, :])[16:32]
    above = column(above.astype(F32)[SLOTS - 1 : SLOTS, :])[0:16]
    label = jnp.concatenate(
        [
            iota((128, 128), 0, F32),
            jnp.where(here > 0, below + 128.0, -7.0),
            jnp.where(here < owners - 1, above + 256.0, -7.0),
            jnp.full((96, 128), -7.0, F32),
        ],
        axis=0,
    )
    label = jnp.concatenate([label] * (total // 128), axis=1)
    table = hot(label == key)
    part[0:160, :] = dot(table[0:160], got[...]).astype(BF)
    counted = dot(
        jnp.concatenate([fact(1), fact(2), jnp.zeros((6, total), F32)], axis=0).astype(BF),
        table,
        NT,
    )
    count = counted[0:1] * 16.0 + counted[1:2]
    third = jnp.floor(count / 65536.0)
    second = jnp.floor((count - 65536.0 * third) / 256.0)
    first = count - 65536.0 * third - 256.0 * second
    digits = [first, second, third]
    part[160:176, :] = jnp.concatenate(
        [d[:, 0:128] for d in digits]
        + [d[:, 128:256] for d in digits]
        + [jnp.zeros((10, 128), F32)],
        axis=0,
    ).astype(BF)
    slot = iota((CAP * owners, owners), 0)
    ids = dot(hot(slot // CAP == iota((CAP * owners, owners), 1)), metas[0:owners])
    lanes = iota((CAP * owners, 128), 1)
    turns = iota((CAP * owners, 128), 0) % CAP
    named = jnp.sum(jnp.where(lanes == turns, ids, 0.0), axis=1, keepdims=True)
    back[...] = hot(lanes.astype(F32) == named)


def coarse_kernel(layer, own, other1, other2, other3, back, weights, src, dst, out, reply):
    w = [weights[layer, i] for i in range(6)]
    whole = (own[...].astype(F32) + other1[...].astype(F32)) + (
        other2[...].astype(F32) + other3[...].astype(F32)
    )

    def counts(first):
        row = (
            whole[first : first + 1]
            + 256.0 * whole[first + 1 : first + 2]
            + 65536.0 * whole[first + 2 : first + 3]
        )
        return jnp.maximum(column(row), 1.0)

    rows = (whole[0:128] / counts(160)).astype(BF)
    ghosts = (whole[128:160] / counts(163)[0:32]).astype(BF)
    table = jnp.concatenate([rows, ghosts], axis=0)
    source = dot(w[0] * BF(0.5), table, (((0,), (1,)), ((), ()))).astype(BF)
    target = dot(w[1] * BF(0.5), rows, (((0,), (1,)), ((), ()))).astype(BF)
    from_hot = rows_hot(src[...], 160)
    to_hot = rows_hot(dst[...], 128)
    half = dot(source, from_hot) + dot(target, to_hot)
    sums = dot(to_hot, half_silu(half).astype(BF), NT).astype(BF)
    new = node_update(rows, sums, *node_weights(w))
    out[...] = new
    reply[...] = dot(back[...], new).astype(BF)


def lift_kernel(place, rows_ref, cluster, slot_of, reply, lists, out, near, far):
    row_count = rows_ref.shape[0]
    by_cluster = dot(slot_of[...], reply[...]).astype(BF)
    lanes = iota((128, 128), 1, F32)
    for first in range(0, row_count, 128):
        member = hot(column(cluster[:, first : first + 128]) == lanes)
        at = pl.ds(first, 128)
        out[at, :] = (rows_ref[at, :].astype(F32) + dot(member, by_cluster)).astype(BF)
    pick_both(out, lists, place[1] % 2 == 1, near, far)


def run(kernel, outs, args, scalars=0, layer=None, scratch=(), flops=0, name=None):
    specs = []
    for i, arg in enumerate(args):
        if i < scalars:
            specs.append(pl.BlockSpec(memory_space=pltpu.SMEM))
        else:
            specs.append(pl.BlockSpec(memory_space=pltpu.VMEM))
    return pl.pallas_call(
        kernel if layer is None else functools.partial(kernel, layer),
        out_shape=[jax.ShapeDtypeStruct(shape, BF) for shape in outs],
        in_specs=specs,
        out_specs=[pl.BlockSpec(memory_space=pltpu.VMEM) for _ in outs],
        scratch_shapes=[pltpu.VMEM(shape, BF) for shape in scratch],
        compiler_params=pltpu.CompilerParams(vmem_limit_bytes=VMEM_LIMIT),
        cost_estimate=pl.CostEstimate(flops=flops, bytes_accessed=1 << 20, transcendentals=0),
        name=name,
    )(*args)


def on_device(
    nodes,
    weights,
    edge_src,
    edge_dst,
    edge_valid,
    ghost_list,
    cluster_of,
    owner,
    coarse_row,
    coarse_src,
    coarse_dst,
    coarse_ghosts,
):
    count, width = nodes.shape
    doms, subs = lax.axis_size("dom"), lax.axis_size("sub")
    place = jnp.stack([lax.axis_index("dom"), lax.axis_index("sub")]).astype(I32)
    lists = ghost_list[0]
    owner = owner.reshape(1, -1)
    coarse_lists = coarse_ghosts.reshape(1, -1)
    edges = (edge_src, edge_dst, edge_valid)
    ghost = (GH, width)
    chain = doms * subs
    near_pairs = [(i, i ^ 1) for i in range(chain)]
    far_pairs = [(i, i + 1 if i % 2 else i - 1) for i in range(1, chain - 1)]

    def swap(near, far):
        from_far = lax.ppermute(far, ("dom", "sub"), far_pairs)
        from_near = lax.ppermute(near, ("dom", "sub"), near_pairs)
        return from_near, from_far

    def inner(states, layer):
        return run(
            inner_kernel,
            [states.shape],
            (states, weights) + edges,
            layer=layer,
            scratch=[(width, count), (width, count), (count, width)],
            flops=5 * 10**9,
            name="inner",
        )[0]

    near, far = run(pick_kernel, [ghost, ghost], (place, nodes, lists), scalars=1, name="pick")
    ghosts = swap(near, far)
    slot_pick, facts, slot_of = run(
        prepare_kernel,
        [(doms * SLOTS, 256), (128, 128), (128, CAP * doms)],
        (cluster_of, owner, coarse_row, coarse_lists),
        flops=10**8,
        name="prepare",
    )
    middle = inner(nodes, 0)
    first, near, far = run(
        ends_pick_kernel,
        [nodes.shape, ghost, ghost],
        (place, nodes, middle) + ghosts + (weights,) + edges + (lists,),
        scalars=1,
        layer=0,
        flops=10**9,
        name="ends_pick",
    )
    ghosts = swap(near, far)
    middle = inner(first, 1)
    second, parcel = run(
        ends_pool_kernel,
        [nodes.shape, (doms * SLOTS, width)],
        (place, first, middle) + ghosts + (weights,) + edges + (cluster_of, slot_pick, facts),
        scalars=1,
        layer=1,
        flops=10**9,
        name="ends_pool",
    )
    got = lax.all_to_all(
        parcel.reshape(doms, SLOTS, width), "dom", split_axis=0, concat_axis=0, tiled=True
    ).reshape(doms * SLOTS, width)
    part, back = run(
        received_kernel,
        [(176, width), (doms * CAP, width)],
        (place, got),
        scalars=1,
        flops=10**8,
        name="received",
    )
    others = [lax.ppermute(part, "sub", [(i, i ^ k) for i in range(subs)]) for k in (1, 2, 3)]
    coarse, reply = run(
        coarse_kernel,
        [(128, width), (doms * CAP, width)],
        (part, *others, back, weights, coarse_src, coarse_dst),
        layer=2,
        flops=10**9,
        name="coarse",
    )
    reply = lax.all_to_all(
        reply.reshape(doms, CAP, width), "dom", split_axis=0, concat_axis=0, tiled=True
    ).reshape(doms * CAP, width)
    lifted, near, far = run(
        lift_kernel,
        [nodes.shape, ghost, ghost],
        (place, second, cluster_of, slot_of, reply, lists),
        scalars=1,
        flops=10**9,
        name="lift",
    )
    ghosts = swap(near, far)
    middle = inner(lifted, 3)
    (last,) = run(
        ends_kernel,
        [nodes.shape],
        (place, lifted, middle) + ghosts + (weights,) + edges,
        scalars=1,
        layer=3,
        flops=10**9,
        name="ends",
    )
    return (last, coarse)


def solution(mesh):
    placed = (
        P(("dom", "sub"), None),
        P(),
        P(("dom", "sub"), None),
        P(("dom", "sub"), None),
        P(("dom", "sub"), None),
        P(("dom", "sub"), None, None),
        P(("dom", "sub"), None),
        P(("dom", "sub"), None, None),
        P(("dom", "sub"), None),
        P("dom", None),
        P("dom", None),
        P("dom", None, None),
    )
    return jax.shard_map(
        on_device,
        mesh=mesh,
        in_specs=placed,
        out_specs=(P(("dom", "sub"), None), P("dom", None)),
        check_vma=False,
    )
```

```python
import functools

import jax
import jax.numpy as jnp
from jax import lax
from jax.experimental import pallas as pl
from jax.experimental.pallas import tpu as pltpu
from jax.sharding import PartitionSpec as P

BF = jnp.bfloat16
F32 = jnp.float32
I32 = jnp.int32
I16 = jnp.int16
NN = (((1,), (0,)), ((), ()))
NT = (((1,), (1,)), ((), ()))
TN = (((0,), (0,)), ((), ()))

GH = 128
CAP = 4
SLOTS = 16
VMEM_LIMIT = 28 << 20


def dot(left, right, dims=NN):
    return lax.dot_general(left, right, dims, preferred_element_type=F32)


def iota(shape, dim, dtype=I32):
    return lax.broadcasted_iota(I32, shape, dim).astype(dtype)


def hot(mask):
    return jnp.where(mask, 1.0, 0.0).astype(BF)


def column(row):
    return jnp.broadcast_to(row.astype(F32), (128, 128)).T


def half_silu(half):
    return half * (1.0 + jnp.tanh(half))


def rows_hot(index_row, count):
    table = lax.broadcasted_iota(I16, (count, index_row.shape[1]), 0)
    return jnp.where(table == index_row.astype(I16), BF(1), BF(0))


def edge_sum(source_t, target_t, from_hot, to_hot):
    table = jnp.concatenate([source_t, target_t], axis=1)
    half = dot(table, jnp.concatenate([from_hot, to_hot], axis=0))
    return dot(half_silu(half).astype(BF), to_hot, NT).astype(BF)


def layer_weights(w):
    first = jnp.concatenate([w[0].astype(F32).T, w[1].astype(F32).T], axis=0) * 0.5
    both = jnp.concatenate([w[3].astype(F32).T, dot(w[2], w[4]).T], axis=1) * 0.5
    last = w[5].astype(F32)
    last = last - jnp.mean(last, axis=1, keepdims=True)
    return first.astype(BF), both.astype(BF), last.T.astype(BF)


def node_update(rows_t, sums_t, both, last):
    half = dot(both, jnp.concatenate([rows_t, sums_t], axis=0))
    centred = dot(last, half_silu(half).astype(BF))
    spread = jnp.mean(centred * centred, axis=0, keepdims=True)
    return (rows_t.astype(F32) + centred * lax.rsqrt(spread + 1e-5)).astype(BF)


def local_edges(b, row_count, src, dst, valid, width):
    at = pl.ds(b * width, width)
    edge = src[:, at]
    line = jnp.where(
        edge < row_count, edge + GH, jnp.where(edge < row_count + GH, edge - row_count, edge)
    )
    to_row = jnp.where(valid[:, at] != 0, dst[:, at] - b * GH, -1)
    return rows_hot(line - b * GH, 3 * GH), rows_hot(to_row, GH)


def pick_both(rows_t, lists, odd, near, far):
    to_lower, to_upper = lists[0:1, :], lists[1:2, :]
    wanted = jnp.concatenate(
        [jnp.where(odd, to_lower, to_upper), jnp.where(odd, to_upper, to_lower)], axis=1
    )
    picked = dot(rows_t[...], rows_hot(wanted, rows_t.shape[1])).astype(BF)
    near[...] = picked[:, :GH]
    far[...] = picked[:, GH:]


def inner_kernel(layer, rows_t, weights, src, dst, valid, out, first, both, last, ends, sums):
    row_count = rows_t.shape[1]
    blocks = row_count // GH
    width = src.shape[1] // blocks
    first[...], both[...], last[...] = layer_weights([weights[layer, i] for i in range(6)])
    ends[...] = dot(first[...], rows_t[...]).astype(BF)
    for b in range(1, blocks - 1):
        at = slice(b * GH, (b + 1) * GH)
        sums[:, at] = edge_sum(
            ends[0:128, (b - 1) * GH : (b + 2) * GH],
            ends[128:256, at],
            *local_edges(b, row_count, src, dst, valid, width),
        )
    step = (row_count - 2 * GH) // 2
    for start in range(GH, row_count - GH, step):
        at = slice(start, start + step)
        out[:, at] = node_update(rows_t[:, at], sums[:, at], both[...], last[...])


def end_blocks(place, rows_t, from_near, from_far, first, both, last, src, dst, valid):
    odd = place[1] % 2 == 1
    row_count = rows_t.shape[1]
    blocks = row_count // GH
    width = src.shape[1] // blocks
    near, far = from_near[...], from_far[...]
    nothing = jnp.zeros_like(near)
    before = jnp.where(place[2] == 0, nothing, jnp.where(odd, near, far))
    after = jnp.where(place[3] == 0, nothing, jnp.where(odd, far, near))
    head, tail = rows_t[:, 0 : 2 * GH], rows_t[:, row_count - 2 * GH :]
    line = jnp.concatenate([before, head, tail, after], axis=1)
    ends = dot(first[...], line).astype(BF)
    sums = [
        edge_sum(
            ends[0:128, at : at + 3 * GH],
            ends[128:256, at + own : at + own + GH],
            *local_edges(b, row_count, src, dst, valid, width),
        )
        for b, at, own in ((0, 0, GH), (blocks - 1, 3 * GH, GH))
    ]
    own = jnp.concatenate([head[:, :GH], tail[:, GH:]], axis=1)
    return node_update(own, jnp.concatenate(sums, axis=1), both[...], last[...])


def whole_layer(inner, new, out):
    count = out.shape[1]
    out[:, GH : count - GH] = inner[:, GH : count - GH]
    out[:, 0:GH] = new[:, :GH]
    out[:, count - GH :] = new[:, GH:]


def ends_kernel(place, inner, *refs):
    out = refs[-1]
    new = end_blocks(place, *refs[:-1])
    count = out.shape[0]
    out[GH : count - GH, :] = inner[:, GH : count - GH].T
    out[0:GH, :] = new[:, :GH].T
    out[count - GH :, :] = new[:, GH:].T


def ends_pick_kernel(place, inner, *refs):
    lists, out, near, far = refs[-4:]
    whole_layer(inner, end_blocks(place, *refs[:-4]), out)
    pick_both(out, lists, place[1] % 2 == 1, near, far)


def ends_pool_kernel(place, inner, *refs):
    cluster, slot_pick, facts, out, parcel = refs[-5:]
    whole_layer(inner, end_blocks(place, *refs[:-5]), out)
    member = rows_hot(cluster[...], 128)
    partial = dot(out[...], member, NT).T.astype(BF)
    parcel[...] = dot(slot_pick[...], jnp.concatenate([partial, facts[...]], axis=0)).astype(BF)


def start_kernel(place, nodes, lists, facts, rows_t, near, far):
    rows_t[...] = nodes[...].T
    pick_both(rows_t, lists, place[1] % 2 == 1, near, far)


def prepare_kernel(cluster, owner, coarse_row, ghosts, slot_pick, facts, slot_of):
    member = rows_hot(cluster[...], 128)
    counts = jnp.sum(member.astype(F32), axis=1, keepdims=True)
    owner_row = owner[...].astype(F32)
    by_row, by_lane = column(owner_row), jnp.broadcast_to(owner_row, (128, 128))
    sub, lane = iota((128, 128), 0), iota((128, 128), 1)
    same = by_row == by_lane
    place_col = jnp.sum(jnp.where(same & (lane < sub), 1.0, 0.0), axis=1, keepdims=True)
    place_row = jnp.sum(jnp.where(same & (sub < lane), 1.0, 0.0), axis=0, keepdims=True)
    slot_row = owner_row * CAP + place_row
    owners = slot_pick.shape[0] // SLOTS
    slot_of[...] = hot(slot_row == iota((CAP * owners, 128), 0, F32))
    row = iota((owners * SLOTS, 128), 0)
    to, at = row // SLOTS, row % SLOTS
    label = jnp.where(
        at < CAP,
        CAP * to + at,
        jnp.where(
            at < 2 * CAP,
            CAP * (to - 1) + at - CAP,
            jnp.where(at < 3 * CAP, CAP * (to + 1) + at - 2 * CAP, -1),
        ),
    )
    slot_pick[:, 0:128] = hot(label.astype(F32) == slot_row)
    fact = jnp.where(
        at == 3 * CAP,
        to,
        jnp.where(
            at == 3 * CAP + 1,
            to - 1,
            jnp.where(at == 3 * CAP + 2, to + 1, jnp.where(at == 3 * CAP + 3, 127, -1)),
        ),
    )
    slot_pick[:, 128:256] = hot(fact == iota(fact.shape, 1))
    high = jnp.floor(counts / 16.0)
    low = counts - 16.0 * high
    lanes = lane.astype(F32)
    values = (
        jnp.where(lanes == place_col, column(coarse_row[...]), 0.0)
        + jnp.where(lanes == place_col + CAP, high, 0.0)
        + jnp.where(lanes == place_col + 2 * CAP, low, 0.0)
    ).astype(BF)
    meta = dot(hot(by_lane == sub.astype(F32)), values)
    each = ghosts.shape[2]
    listed = jnp.concatenate(
        [ghosts[0, 0:1], ghosts[0, 1:2], jnp.zeros((1, 128 - 2 * each), I32)], axis=1
    ).astype(F32)
    facts[...] = jnp.where(sub == 127, listed, meta).astype(BF)


def received_kernel(place, got, part, own_metas):
    total = got.shape[0]
    owners = total // SLOTS
    here = place[0]
    wide = iota((3 * owners, total), 1)
    pick = iota((3 * owners, total), 0)
    metas = dot(
        hot(wide == SLOTS * (pick % owners) + 3 * CAP + pick // owners), got[...]
    ).astype(BF)
    own_metas[...] = metas[0:owners]
    spread = hot((wide // SLOTS == pick % owners) & (wide % SLOTS // CAP == pick // owners))
    facts = dot(metas, spread, TN)[0:16]
    lane = iota((1, total), 1)
    turn = iota((16, total), 0) - iota((16, total), 1) % CAP

    def fact(number):
        return jnp.sum(jnp.where(turn == CAP * number, facts, 0.0), axis=0, keepdims=True)

    group = lane % SLOTS // CAP
    key = jnp.where(group < 3, fact(0) + (128 * group).astype(F32), -1.0)
    below = got[pl.ds(pl.multiple_of(jnp.maximum(here - 1, 0) * SLOTS, SLOTS), SLOTS), :]
    above = got[pl.ds(pl.multiple_of(jnp.minimum(here + 1, owners - 1) * SLOTS, SLOTS), SLOTS), :]
    below = column(below.astype(F32)[SLOTS - 1 : SLOTS, :])[16:32]
    above = column(above.astype(F32)[SLOTS - 1 : SLOTS, :])[0:16]
    label = jnp.concatenate(
        [
            iota((128, 128), 0, F32),
            jnp.where(here > 0, below + 128.0, -7.0),
            jnp.where(here < owners - 1, above + 256.0, -7.0),
            jnp.full((96, 128), -7.0, F32),
        ],
        axis=0,
    )
    label = jnp.concatenate([label] * (total // 128), axis=1)
    table = hot(label == key)
    part[0:160, :] = dot(table[0:160], got[...]).astype(BF)
    counted = dot(
        jnp.concatenate([fact(1), fact(2), jnp.zeros((6, total), F32)], axis=0).astype(BF),
        table,
        NT,
    )
    count = counted[0:1] * 16.0 + counted[1:2]
    third = jnp.floor(count / 65536.0)
    second = jnp.floor((count - 65536.0 * third) / 256.0)
    first = count - 65536.0 * third - 256.0 * second
    digits = [first, second, third]
    part[160:176, :] = jnp.concatenate(
        [d[:, 0:128] for d in digits]
        + [d[:, 128:256] for d in digits]
        + [jnp.zeros((10, 128), F32)],
        axis=0,
    ).astype(BF)


def ready_kernel(layer, own_metas, weights, src, dst, back, first, both, last, from_hot, to_hot):
    owners = own_metas.shape[0]
    slots = CAP * owners
    turn = iota((slots, owners), 0)
    ids = dot(hot(turn // CAP == iota((slots, owners), 1)), own_metas[...])
    lanes = iota((slots, 128), 1)
    turns = iota((slots, 128), 0) % CAP
    named = jnp.sum(jnp.where(lanes == turns, ids, 0.0), axis=1, keepdims=True)
    back[...] = hot(lanes.astype(F32) == named)
    first[...], both[...], last[...] = layer_weights([weights[layer, i] for i in range(6)])
    from_hot[...] = rows_hot(src[...], 160)
    to_hot[...] = rows_hot(dst[...], 128)


def coarse_kernel(own, other1, other2, other3, back, first, both, last, from_hot, to_hot, out, reply):
    whole = (own[...].astype(F32) + other1[...].astype(F32)) + (
        other2[...].astype(F32) + other3[...].astype(F32)
    )

    def counts(at):
        row = whole[at : at + 1] + 256.0 * whole[at + 1 : at + 2] + 65536.0 * whole[at + 2 : at + 3]
        return jnp.maximum(row, 1.0)

    rows_t = (whole[0:128].T / counts(160)).astype(BF)
    ghosts = jnp.concatenate([whole[128:160], jnp.zeros((96, 128), F32)], axis=0)
    ghosts_t = (ghosts.T / counts(163)).astype(BF)
    ends = dot(first[...], jnp.concatenate([rows_t, ghosts_t], axis=1)).astype(BF)
    half = dot(ends[0:128, 0:160], from_hot[...]) + dot(ends[128:256, 0:128], to_hot[...])
    sums = dot(half_silu(half).astype(BF), to_hot[...], NT).astype(BF)
    new = node_update(rows_t, sums, both[...], last[...]).T
    out[...] = new
    reply[...] = dot(back[...], new).astype(BF)


def lift_kernel(place, rows_t, cluster, slot_of, reply, lists, out, near, far):
    by_cluster = dot(reply[...], slot_of[...], TN).astype(BF)
    member = rows_hot(cluster[...], 128)
    out[...] = (rows_t[...].astype(F32) + dot(by_cluster, member)).astype(BF)
    pick_both(out, lists, place[1] % 2 == 1, near, far)


def run(kernel, outs, args, scalars=0, layer=None, scratch=(), flops=0, name=None):
    specs = []
    for i in range(len(args)):
        specs.append(pl.BlockSpec(memory_space=pltpu.SMEM if i < scalars else pltpu.VMEM))
    return pl.pallas_call(
        kernel if layer is None else functools.partial(kernel, layer),
        out_shape=[jax.ShapeDtypeStruct(shape, BF) for shape in outs],
        in_specs=specs,
        out_specs=[pl.BlockSpec(memory_space=pltpu.VMEM) for _ in outs],
        scratch_shapes=scratch,
        compiler_params=pltpu.CompilerParams(vmem_limit_bytes=VMEM_LIMIT),
        cost_estimate=pl.CostEstimate(flops=flops, bytes_accessed=1 << 20, transcendentals=0),
        name=name,
    )(*args)


def on_device(
    nodes,
    weights,
    edge_src,
    edge_dst,
    edge_valid,
    ghost_list,
    cluster_of,
    owner,
    coarse_row,
    coarse_src,
    coarse_dst,
    coarse_ghosts,
):
    count, width = nodes.shape
    doms, subs = lax.axis_size("dom"), lax.axis_size("sub")
    dom, sub = lax.axis_index("dom"), lax.axis_index("sub")
    chain = doms * subs
    index = dom * subs + sub
    place = jnp.stack([dom, sub, index, chain - 1 - index]).astype(I32)
    lists = ghost_list[0]
    edges = (edge_src, edge_dst, edge_valid)
    ghost = (width, GH)
    rows_t = (width, count)
    forms = [(2 * width, width), (width, 2 * width), (width, width)]
    near_pairs = [(i, i ^ 1) for i in range(chain)]
    far_pairs = [(i, (i + 1 if i % 2 else i - 1) % chain) for i in range(chain)]

    def swap(near, far):
        from_near = lax.ppermute(near, ("dom", "sub"), near_pairs)
        from_far = lax.ppermute(far, ("dom", "sub"), far_pairs)
        return from_near, from_far

    def inner(states, layer):
        out, *weights_now = run(
            inner_kernel,
            [rows_t] + forms,
            (states, weights) + edges,
            layer=layer,
            scratch=[pltpu.VMEM((2 * width, count), BF), pltpu.VMEM(rows_t, BF)],
            flops=4 * 10**9,
            name="inner",
        )
        return out, tuple(weights_now)

    slot_pick, facts, slot_of = run(
        prepare_kernel,
        [(doms * SLOTS, 256), (128, 128), (CAP * doms, 128)],
        (cluster_of, owner.reshape(1, -1), coarse_row, coarse_ghosts),
        flops=3 * 10**9,
        name="prepare",
    )
    states, near, far = run(
        start_kernel,
        [rows_t, ghost, ghost],
        (place, nodes, lists, facts),
        scalars=1,
        flops=10**9,
        name="start",
    )
    ghosts = swap(near, far)
    middle, now = inner(states, 0)
    states, near, far = run(
        ends_pick_kernel,
        [rows_t, ghost, ghost],
        (place, middle, states) + ghosts + now + edges + (lists,),
        scalars=1,
        flops=10**9,
        name="ends_pick",
    )
    ghosts = swap(near, far)
    middle, now = inner(states, 1)
    states, parcel = run(
        ends_pool_kernel,
        [rows_t, (doms * SLOTS, width)],
        (place, middle, states) + ghosts + now + edges + (cluster_of, slot_pick, facts),
        scalars=1,
        flops=10**9,
        name="ends_pool",
    )
    got = lax.all_to_all(
        parcel.reshape(doms, SLOTS, width), "dom", split_axis=0, concat_axis=0, tiled=True
    ).reshape(doms * SLOTS, width)
    part, own_metas = run(
        received_kernel,
        [(176, width), (doms, width)],
        (place, got),
        scalars=1,
        flops=10**9,
        name="received",
    )
    others = [lax.ppermute(part, "sub", [(i, i ^ k) for i in range(subs)]) for k in (1, 2, 3)]
    ready = run(
        ready_kernel,
        [(doms * CAP, width)] + forms + [(160, coarse_src.shape[1]), (128, coarse_src.shape[1])],
        (own_metas, weights, coarse_src, coarse_dst),
        layer=2,
        flops=10**9,
        name="ready",
    )
    coarse, reply = run(
        coarse_kernel,
        [(128, width), (doms * CAP, width)],
        (part, *others, *ready),
        flops=10**9,
        name="coarse",
    )
    reply = lax.all_to_all(
        reply.reshape(doms, CAP, width), "dom", split_axis=0, concat_axis=0, tiled=True
    ).reshape(doms * CAP, width)
    states, near, far = run(
        lift_kernel,
        [rows_t, ghost, ghost],
        (place, states, cluster_of, slot_of, reply, lists),
        scalars=1,
        flops=10**9,
        name="lift",
    )
    ghosts = swap(near, far)
    middle, now = inner(states, 3)
    (last,) = run(
        ends_kernel,
        [nodes.shape],
        (place, middle, states) + ghosts + now + edges,
        scalars=1,
        flops=10**9,
        name="ends",
    )
    return (last, coarse)


def solution(mesh):
    placed = (
        P(("dom", "sub"), None),
        P(),
        P(("dom", "sub"), None),
        P(("dom", "sub"), None),
        P(("dom", "sub"), None),
        P(("dom", "sub"), None, None),
        P(("dom", "sub"), None),
        P(("dom", "sub"), None, None),
        P(("dom", "sub"), None),
        P("dom", None),
        P("dom", None),
        P("dom", None, None),
    )
    return jax.shard_map(
        on_device,
        mesh=mesh,
        in_specs=placed,
        out_specs=(P(("dom", "sub"), None), P("dom", None)),
        check_vma=False,
    )
```

```python
import functools

import jax
import jax.numpy as jnp
from jax import lax
from jax.experimental import pallas as pl
from jax.experimental.pallas import tpu as pltpu
from jax.sharding import PartitionSpec as P

BF = jnp.bfloat16
F32 = jnp.float32
I32 = jnp.int32
I16 = jnp.int16
NN = (((1,), (0,)), ((), ()))
NT = (((1,), (1,)), ((), ()))
TN = (((0,), (0,)), ((), ()))

GH = 128
CAP = 4
SLOTS = 16
BACK = 3 * CAP
VMEM_LIMIT = 28 << 20


def dot(left, right, dims=NN):
    return lax.dot_general(left, right, dims, preferred_element_type=F32)


def iota(shape, dim, dtype=I32):
    return lax.broadcasted_iota(I32, shape, dim).astype(dtype)


def hot(mask):
    return jnp.where(mask, 1.0, 0.0).astype(BF)


def column(row):
    return jnp.broadcast_to(row.astype(F32), (128, 128)).T


def half_silu(half):
    return half * (1.0 + jnp.tanh(half))


def rows_hot(index_row, count):
    table = lax.broadcasted_iota(I16, (count, index_row.shape[1]), 0)
    return jnp.where(table == index_row.astype(I16), BF(1), BF(0))


def over_back(row):
    return (row * (65536 // BACK + 1)) >> 16


def edge_sum(source_t, target_t, from_hot, to_hot):
    table = jnp.concatenate([source_t, target_t], axis=1)
    half = dot(table, jnp.concatenate([from_hot, to_hot], axis=0))
    return dot(half_silu(half).astype(BF), to_hot, NT).astype(BF)


def layer_weights(w):
    first = jnp.concatenate([w[0].astype(F32).T, w[1].astype(F32).T], axis=0) * 0.5
    both = jnp.concatenate([w[3].astype(F32).T, dot(w[2], w[4]).T], axis=1) * 0.5
    last = w[5].astype(F32)
    last = last - jnp.mean(last, axis=1, keepdims=True)
    return first.astype(BF), both.astype(BF), last.T.astype(BF)


def node_update(rows_t, sums_t, both, last):
    half = dot(both, jnp.concatenate([rows_t, sums_t], axis=0))
    centred = dot(last, half_silu(half).astype(BF))
    spread = jnp.mean(centred * centred, axis=0, keepdims=True)
    return (rows_t.astype(F32) + centred * lax.rsqrt(spread + 1e-5)).astype(BF)


def local_edges(b, row_count, src, dst, valid, width):
    at = pl.ds(b * width, width)
    edge = src[:, at]
    line = jnp.where(
        edge < row_count, edge + GH, jnp.where(edge < row_count + GH, edge - row_count, edge)
    )
    to_row = jnp.where(valid[:, at] != 0, dst[:, at] - b * GH, -1)
    return rows_hot(line - b * GH, 3 * GH), rows_hot(to_row, GH)


def pick_both(rows_t, lists, odd, near, far):
    to_lower, to_upper = lists[0:1, :], lists[1:2, :]
    wanted = jnp.concatenate(
        [jnp.where(odd, to_lower, to_upper), jnp.where(odd, to_upper, to_lower)], axis=1
    )
    picked = dot(rows_t[...], rows_hot(wanted, rows_t.shape[1])).astype(BF)
    near[0 : picked.shape[0], :] = picked[:, :GH]
    far[0 : picked.shape[0], :] = picked[:, GH:]


def inner_kernel(layer, rows_t, weights, src, dst, valid, out, first, both, last, ends, sums):
    row_count = rows_t.shape[1]
    blocks = row_count // GH
    width = src.shape[1] // blocks
    first[...], both[...], last[...] = layer_weights([weights[layer, i] for i in range(6)])
    ends[...] = dot(first[...], rows_t[...]).astype(BF)
    for b in range(1, blocks - 1):
        at = slice(b * GH, (b + 1) * GH)
        sums[:, at] = edge_sum(
            ends[0:128, (b - 1) * GH : (b + 2) * GH],
            ends[128:256, at],
            *local_edges(b, row_count, src, dst, valid, width),
        )
    step = (row_count - 2 * GH) // 2
    for start in range(GH, row_count - GH, step):
        at = slice(start, start + step)
        out[:, at] = node_update(rows_t[:, at], sums[:, at], both[...], last[...])


def by_side(place, near, far):
    odd = place[1] % 2 == 1
    return jnp.where(odd, near, far), jnp.where(odd, far, near)


def ghost_rows(place, before, after):
    nothing = jnp.zeros_like(before)
    return jnp.where(place[2] == 0, nothing, before), jnp.where(place[3] == 0, nothing, after)


def end_blocks(place, rows_t, from_near, from_far, first, both, last, src, dst, valid, turn=False):
    row_count = rows_t.shape[1]
    blocks = row_count // GH
    width = src.shape[1] // blocks
    before, after = by_side(place, from_near[0:128, :], from_far[0:128, :])
    before, after = ghost_rows(place, before, after)
    if turn:
        before, after = before.T, after.T
    head, tail = rows_t[:, 0 : 2 * GH], rows_t[:, row_count - 2 * GH :]
    line = jnp.concatenate([before, head, tail, after], axis=1)
    ends = dot(first[...], line).astype(BF)
    sums = [
        edge_sum(
            ends[0:128, at : at + 3 * GH],
            ends[128:256, at + own : at + own + GH],
            *local_edges(b, row_count, src, dst, valid, width),
        )
        for b, at, own in ((0, 0, GH), (blocks - 1, 3 * GH, GH))
    ]
    own = jnp.concatenate([head[:, :GH], tail[:, GH:]], axis=1)
    return node_update(own, jnp.concatenate(sums, axis=1), both[...], last[...])


def whole_layer(inner, new, out):
    count = out.shape[1]
    out[:, GH : count - GH] = inner[:, GH : count - GH]
    out[:, 0:GH] = new[:, :GH]
    out[:, count - GH :] = new[:, GH:]


def ends_pick_kernel(place, inner, *refs):
    lists, cluster, facts, slot_row, out, near, far, more = refs[-8:]
    slots = dot(slot_row[...], rows_hot(cluster[...], 128)).astype(BF)
    whole_layer(inner, end_blocks(place, *refs[:-8], turn=True), out)
    more[0:128, :] = out[...]
    more[128:144, :] = slots
    pick_both(more, lists, place[1] % 2 == 1, near, far)
    near[144:208, :] = facts[0:64, :]
    far[144:208, :] = facts[0:64, :]


def ends_pool_kernel(place, inner, *refs):
    cluster, slot_pick, facts, out, parcel = refs[-5:]
    whole_layer(inner, end_blocks(place, *refs[:-5]), out)
    member = rows_hot(cluster[...], 128)
    partial = dot(out[...], member, NT).T.astype(BF)
    ids = by_side(place, refs[1][144:208, :], refs[2][144:208, :])
    lane = iota(ids[0].shape, 1)
    moved = [pltpu.roll(ids[side].astype(F32), CAP * (3 + side), 1) for side in (0, 1)]
    moved = [jnp.where(lane // CAP == 3 + side, moved[side], 0.0) for side in (0, 1)]
    added = moved[0] + moved[1]
    known = jnp.concatenate([added, jnp.zeros_like(added)], axis=0) + facts[...].astype(F32)
    parcel[...] = dot(
        slot_pick[...], jnp.concatenate([partial, known.astype(BF)], axis=0)
    ).astype(BF)


def turn_kernel(nodes, rows_t):
    rows_t[...] = nodes[...].T


def pick_kernel(place, rows_t, lists, near, far):
    pick_both(rows_t, lists, place[1] % 2 == 1, near, far)


def prepare_kernel(cluster, owner, coarse_row, ghosts, slot_pick, facts, slot_of, slot_row_out):
    member = rows_hot(cluster[...], 128)
    counts = jnp.sum(member.astype(F32), axis=1, keepdims=True)
    owner_row = owner[...].astype(F32)
    by_row, by_lane = column(owner_row), jnp.broadcast_to(owner_row, (128, 128))
    sub, lane = iota((128, 128), 0), iota((128, 128), 1)
    same = by_row == by_lane
    place_col = jnp.sum(jnp.where(same & (lane < sub), 1.0, 0.0), axis=1, keepdims=True)
    place_row = jnp.sum(jnp.where(same & (sub < lane), 1.0, 0.0), axis=0, keepdims=True)
    slot_row = owner_row * CAP + place_row
    owners = slot_pick.shape[0] // SLOTS
    slot_row_out[...] = jnp.broadcast_to(slot_row, slot_row_out.shape).astype(BF)
    row = iota((owners * SLOTS, 128), 0)
    to, at = row // SLOTS, row % SLOTS
    label = jnp.where(
        at < CAP,
        CAP * to + at,
        jnp.where(
            at < 2 * CAP,
            CAP * (to - 1) + at - CAP,
            jnp.where(at < 3 * CAP, CAP * (to + 1) + at - 2 * CAP, -1),
        ),
    )
    slot_pick[:, 0:128] = hot(label.astype(F32) == slot_row)
    back_row = iota(slot_of.shape, 0)
    back_to = over_back(back_row)
    back_at = back_row - BACK * back_to
    slot_of[...] = hot(
        jnp.where(back_at < CAP, CAP * back_to + back_at, -1).astype(F32) == slot_row
    )
    fact = jnp.where(
        at == 3 * CAP,
        to,
        jnp.where(
            at == 3 * CAP + 1,
            to - 1,
            jnp.where(at == 3 * CAP + 2, to + 1, jnp.where(at == 3 * CAP + 3, 127, -1)),
        ),
    )
    slot_pick[:, 128:256] = hot(fact == iota(fact.shape, 1))
    high = jnp.floor(counts / 16.0)
    low = counts - 16.0 * high
    lanes = lane.astype(F32)
    values = (
        jnp.where(lanes == place_col, column(coarse_row[...]), 0.0)
        + jnp.where(lanes == place_col + CAP, high, 0.0)
        + jnp.where(lanes == place_col + 2 * CAP, low, 0.0)
    ).astype(BF)
    meta = dot(hot(by_lane == sub.astype(F32)), values)
    each = ghosts.shape[2]
    listed = jnp.concatenate(
        [ghosts[0, 0:1], ghosts[0, 1:2], jnp.zeros((1, 128 - 2 * each), I32)], axis=1
    ).astype(F32)
    facts[...] = jnp.where(sub == 127, listed, meta).astype(BF)


def received_kernel(place, got, part, own_metas):
    total = got.shape[0]
    owners = total // SLOTS
    here = place[0]
    wide = iota((3 * owners, total), 1)
    pick = iota((3 * owners, total), 0)
    metas = dot(
        hot(wide == SLOTS * (pick % owners) + 3 * CAP + pick // owners), got[...]
    ).astype(BF)
    own_metas[...] = metas[0:owners]
    spread = hot((wide // SLOTS == pick % owners) & (wide % SLOTS // CAP == pick // owners))
    facts = dot(metas, spread, TN)[0:16]
    lane = iota((1, total), 1)
    turn = iota((16, total), 0) - iota((16, total), 1) % CAP

    def fact(number):
        return jnp.sum(jnp.where(turn == CAP * number, facts, 0.0), axis=0, keepdims=True)

    group = lane % SLOTS // CAP
    key = jnp.where(group < 3, fact(0) + (128 * group).astype(F32), -1.0)
    below = got[pl.ds(pl.multiple_of(jnp.maximum(here - 1, 0) * SLOTS, SLOTS), SLOTS), :]
    above = got[pl.ds(pl.multiple_of(jnp.minimum(here + 1, owners - 1) * SLOTS, SLOTS), SLOTS), :]
    below = column(below.astype(F32)[SLOTS - 1 : SLOTS, :])[16:32]
    above = column(above.astype(F32)[SLOTS - 1 : SLOTS, :])[0:16]
    label = jnp.concatenate(
        [
            iota((128, 128), 0, F32),
            jnp.where(here > 0, below + 128.0, -7.0),
            jnp.where(here < owners - 1, above + 256.0, -7.0),
            jnp.full((96, 128), -7.0, F32),
        ],
        axis=0,
    )
    label = jnp.concatenate([label] * (total // 128), axis=1)
    table = hot(label == key)
    part[0:160, :] = dot(table[0:160], got[...]).astype(BF)
    counted = dot(
        jnp.concatenate([fact(1), fact(2), jnp.zeros((6, total), F32)], axis=0).astype(BF),
        table,
        NT,
    )
    count = counted[0:1] * 16.0 + counted[1:2]
    third = jnp.floor(count / 65536.0)
    second = jnp.floor((count - 65536.0 * third) / 256.0)
    first = count - 65536.0 * third - 256.0 * second
    digits = [first, second, third]
    part[160:176, :] = jnp.concatenate(
        [d[:, 0:128] for d in digits]
        + [d[:, 128:256] for d in digits]
        + [jnp.zeros((10, 128), F32)],
        axis=0,
    ).astype(BF)


def ready_kernel(own_metas, weights, src, dst, near, far, *outs):
    back, first, both, last, from_hot, to_hot, first3, both3, last3 = outs
    owners = own_metas.shape[0]
    total = BACK * owners
    ids = dot(hot(over_back(iota((total, owners), 0)) == iota((total, owners), 1)), own_metas[...])
    row = iota((total, 128), 0)
    at = row - BACK * over_back(row)
    lanes = iota((total, 128), 1)
    wanted = jnp.where(at < CAP, at, at + 2 * CAP)
    named = jnp.sum(jnp.where(lanes == wanted, ids, 0.0), axis=1, keepdims=True)
    back[...] = hot(lanes.astype(F32) == named)
    first[...], both[...], last[...] = layer_weights([weights[2, i] for i in range(6)])
    first3[...], both3[...], last3[...] = layer_weights([weights[3, i] for i in range(6)])
    from_hot[...] = rows_hot(src[...], 160)
    to_hot[...] = rows_hot(dst[...], 128)


def coarse_kernel(own, other1, other2, other3, back, first, both, last, from_hot, to_hot, out, reply):
    whole = (own[...].astype(F32) + other1[...].astype(F32)) + (
        other2[...].astype(F32) + other3[...].astype(F32)
    )

    def counts(at):
        row = whole[at : at + 1] + 256.0 * whole[at + 1 : at + 2] + 65536.0 * whole[at + 2 : at + 3]
        return jnp.maximum(row, 1.0)

    rows_t = (whole[0:128].T / counts(160)).astype(BF)
    ghosts = jnp.concatenate([whole[128:160], jnp.zeros((96, 128), F32)], axis=0)
    ghosts_t = (ghosts.T / counts(163)).astype(BF)
    ends = dot(first[...], jnp.concatenate([rows_t, ghosts_t], axis=1)).astype(BF)
    half = dot(ends[0:128, 0:160], from_hot[...]) + dot(ends[128:256, 0:128], to_hot[...])
    sums = dot(half_silu(half).astype(BF), to_hot[...], NT).astype(BF)
    new = node_update(rows_t, sums, both[...], last[...]).T
    out[...] = new
    reply[...] = dot(back[...], new).astype(BF)


def final_kernel(
    place,
    rows_t,
    reply,
    slot_of,
    cluster,
    early_near,
    early_far,
    from_near,
    from_far,
    first,
    both,
    last,
    src,
    dst,
    valid,
    out,
    line,
    ends,
    sums,
):
    row_count = rows_t.shape[1]
    blocks = row_count // GH
    width = src.shape[1] // blocks
    tables = [slot_of[...]]
    for at, slots in enumerate(by_side(place, early_near[128:144, :], early_far[128:144, :])):
        slot = slots.astype(F32).astype(I32)[0:1]
        tables.append(rows_hot(slot // CAP * BACK + slot % CAP + CAP * (at + 1), reply.shape[0]))
    coarse = dot(reply[...], jnp.concatenate(tables, axis=1), TN)
    member = rows_hot(cluster[...], 128)
    before, after = by_side(place, from_near[...], from_far[...])
    before = (before.astype(F32) + coarse[:, 128:256]).astype(BF)
    after = (after.astype(F32) + coarse[:, 256:384]).astype(BF)
    line[:, 0:GH], line[:, GH + row_count :] = ghost_rows(place, before, after)
    line[:, GH : GH + row_count] = (
        rows_t[...].astype(F32) + dot(coarse[:, 0:128].astype(BF), member)
    ).astype(BF)
    ends[...] = dot(first[...], line[...]).astype(BF)
    for b in range(blocks):
        sums[:, b * GH : (b + 1) * GH] = edge_sum(
            ends[0:128, b * GH : (b + 3) * GH],
            ends[128:256, (b + 1) * GH : (b + 2) * GH],
            *local_edges(b, row_count, src, dst, valid, width),
        )
    step = row_count // 2
    for start in range(0, row_count, step):
        own = line[:, GH + start : GH + start + step]
        new = node_update(own, sums[:, start : start + step], both[...], last[...])
        out[start : start + step, :] = new.T


def run(kernel, outs, args, scalars=0, layer=None, scratch=(), flops=0, name=None):
    specs = []
    for i in range(len(args)):
        specs.append(pl.BlockSpec(memory_space=pltpu.SMEM if i < scalars else pltpu.VMEM))
    return pl.pallas_call(
        kernel if layer is None else functools.partial(kernel, layer),
        out_shape=[jax.ShapeDtypeStruct(shape, BF) for shape in outs],
        in_specs=specs,
        out_specs=[pl.BlockSpec(memory_space=pltpu.VMEM) for _ in outs],
        scratch_shapes=scratch,
        compiler_params=pltpu.CompilerParams(vmem_limit_bytes=VMEM_LIMIT),
        cost_estimate=pl.CostEstimate(flops=flops, bytes_accessed=1 << 20, transcendentals=0),
        name=name,
    )(*args)


def on_device(
    nodes,
    weights,
    edge_src,
    edge_dst,
    edge_valid,
    ghost_list,
    cluster_of,
    owner,
    coarse_row,
    coarse_src,
    coarse_dst,
    coarse_ghosts,
):
    count, width = nodes.shape
    doms, subs = lax.axis_size("dom"), lax.axis_size("sub")
    dom, sub = lax.axis_index("dom"), lax.axis_index("sub")
    chain = doms * subs
    index = dom * subs + sub
    place = jnp.stack([dom, sub, index, chain - 1 - index]).astype(I32)
    lists = ghost_list[0]
    edges = (edge_src, edge_dst, edge_valid)
    ghost = (width, GH)
    rows_t = (width, count)
    forms = [(2 * width, width), (width, 2 * width), (width, width)]
    near_pairs = [(i, i ^ 1) for i in range(chain)]
    far_pairs = [(i, (i + 1 if i % 2 else i - 1) % chain) for i in range(chain)]

    def swap(near, far):
        from_near = lax.ppermute(near, ("dom", "sub"), near_pairs)
        from_far = lax.ppermute(far, ("dom", "sub"), far_pairs)
        return from_near, from_far

    def inner(states, layer):
        out, *weights_now = run(
            inner_kernel,
            [rows_t] + forms,
            (states, weights) + edges,
            layer=layer,
            scratch=[pltpu.VMEM((2 * width, count), BF), pltpu.VMEM(rows_t, BF)],
            flops=4 * 10**9,
            name="inner",
        )
        return out, tuple(weights_now)

    wanted = lists.reshape(-1, 1) == jnp.arange(count, dtype=I32)[None, :]
    picked = dot(wanted.astype(BF), nodes).astype(BF)
    odd = sub % 2 == 1
    ghosts = swap(
        jnp.where(odd, picked[:GH], picked[GH:]), jnp.where(odd, picked[GH:], picked[:GH])
    )
    (states,) = run(turn_kernel, [rows_t], (nodes,), flops=3 * 10**8, name="turn")
    slot_pick, facts, slot_of, slot_row = run(
        prepare_kernel,
        [(doms * SLOTS, 256), (128, 128), (doms * BACK, 128), (16, 128)],
        (cluster_of, owner.reshape(1, -1), coarse_row, coarse_ghosts),
        flops=10**9,
        name="prepare",
    )
    middle, now = inner(states, 0)
    early = (GH + 16 + doms, GH)
    states, near, far = run(
        ends_pick_kernel,
        [rows_t, early, early],
        (place, middle, states) + ghosts + now + edges + (lists, cluster_of, facts, slot_row),
        scalars=1,
        scratch=[pltpu.VMEM((width + 16, count), BF)],
        flops=10**9,
        name="ends_pick",
    )
    early = swap(near, far)
    middle, now = inner(states, 1)
    states, parcel = run(
        ends_pool_kernel,
        [rows_t, (doms * SLOTS, width)],
        (place, middle, states) + early + now + edges + (cluster_of, slot_pick, facts),
        scalars=1,
        flops=10**9,
        name="ends_pool",
    )
    ghosts = swap(
        *run(pick_kernel, [ghost, ghost], (place, states, lists), scalars=1, flops=10**9, name="pick")
    )

    def exchange(rows):
        shape = rows.shape
        rows = rows.reshape(doms, shape[0] // doms, width)
        rows = lax.all_to_all(rows, "dom", split_axis=0, concat_axis=0, tiled=True)
        return rows.reshape(shape)

    part, own_metas = run(
        received_kernel,
        [(176, width), (doms, width)],
        (place, exchange(parcel)),
        scalars=1,
        flops=10**9,
        name="received",
    )
    others = {
        k: lax.ppermute(part, "sub", [(i, i ^ k) for i in range(subs)]) for k in (1, 3, 2)
    }
    back, *ready = run(
        ready_kernel,
        [(doms * BACK, width)]
        + forms
        + [(160, coarse_src.shape[1]), (128, coarse_src.shape[1])]
        + forms,
        (own_metas, weights, coarse_src, coarse_dst) + ghosts,
        flops=10**9,
        name="ready",
    )
    coarse, reply = run(
        coarse_kernel,
        [(128, width), (doms * BACK, width)],
        (part, others[1], others[2], others[3], back, *ready[:5]),
        flops=10**9,
        name="coarse",
    )
    (last,) = run(
        final_kernel,
        [nodes.shape],
        (place, states, exchange(reply), slot_of, cluster_of) + early + ghosts + tuple(ready[5:8]) + edges,
        scalars=1,
        scratch=[
            pltpu.VMEM((width, count + 2 * GH), BF),
            pltpu.VMEM((2 * width, count + 2 * GH), BF),
            pltpu.VMEM(rows_t, BF),
        ],
        flops=5 * 10**9,
        name="final",
    )
    return (last, coarse)


def solution(mesh):
    placed = (
        P(("dom", "sub"), None),
        P(),
        P(("dom", "sub"), None),
        P(("dom", "sub"), None),
        P(("dom", "sub"), None),
        P(("dom", "sub"), None, None),
        P(("dom", "sub"), None),
        P(("dom", "sub"), None, None),
        P(("dom", "sub"), None),
        P("dom", None),
        P("dom", None),
        P("dom", None, None),
    )
    return jax.shard_map(
        on_device,
        mesh=mesh,
        in_specs=placed,
        out_specs=(P(("dom", "sub"), None), P("dom", None)),
        check_vma=False,
    )
```

```python
import functools

import jax
import jax.numpy as jnp
from jax import lax
from jax.experimental import pallas as pl
from jax.experimental.pallas import tpu as pltpu
from jax.sharding import PartitionSpec as P

BF = jnp.bfloat16
F32 = jnp.float32
I32 = jnp.int32
I16 = jnp.int16
NN = (((1,), (0,)), ((), ()))
NT = (((1,), (1,)), ((), ()))
TN = (((0,), (0,)), ((), ()))

GH = 128
CAP = 4
SLOTS = 16
BACK = 3 * CAP
VMEM_LIMIT = 28 << 20
FINAL_PARTS = 2


def dot(left, right, dims=NN):
    return lax.dot_general(left, right, dims, preferred_element_type=F32)


def iota(shape, dim, dtype=I32):
    return lax.broadcasted_iota(I32, shape, dim).astype(dtype)


def hot(mask):
    return jnp.where(mask, 1.0, 0.0).astype(BF)


def column(row):
    return jnp.broadcast_to(row.astype(F32), (128, 128)).T


def half_silu(half):
    return half * (1.0 + jnp.tanh(half))


def rows_hot(index_row, count):
    table = lax.broadcasted_iota(I16, (count, index_row.shape[1]), 0)
    return jnp.where(table == index_row.astype(I16), BF(1), BF(0))


def over_back(row):
    return (row * (65536 // BACK + 1)) >> 16


def edge_halves(source_t, target_t, from_hot, to_hot):
    table = jnp.concatenate([source_t, target_t], axis=1)
    return dot(table, jnp.concatenate([from_hot, to_hot], axis=0)), to_hot


def edge_sum(half, to_hot):
    return dot(half_silu(half).astype(BF), to_hot, NT).astype(BF)


def edge_sums(first, last, halves, sums):
    ahead = halves(first)
    for b in range(first, last):
        now, ahead = ahead, halves(b + 1) if b + 1 < last else None
        sums[:, b * GH : (b + 1) * GH] = edge_sum(*now)


def layer_weights(w):
    first = jnp.concatenate([w[0].astype(F32).T, w[1].astype(F32).T], axis=0) * 0.5
    both = jnp.concatenate([w[3].astype(F32).T, dot(w[2], w[4]).T], axis=1) * 0.5
    last = w[5].astype(F32)
    last = last - jnp.mean(last, axis=1, keepdims=True)
    return first.astype(BF), both.astype(BF), last.T.astype(BF)


def node_updates(pieces, both, last):
    halves = [dot(both, jnp.concatenate(piece, axis=0)) for piece in pieces]
    centred = [dot(last, half_silu(half).astype(BF)) for half in halves]
    new = []
    for (rows_t, _), piece in zip(pieces, centred):
        spread = jnp.mean(piece * piece, axis=0, keepdims=True)
        new.append((rows_t.astype(F32) + piece * lax.rsqrt(spread + 1e-5)).astype(BF))
    return new


def local_edges(b, row_count, src, dst, valid, width):
    at = pl.ds(b * width, width)
    edge = src[:, at]
    line = jnp.where(
        edge < row_count, edge + GH, jnp.where(edge < row_count + GH, edge - row_count, edge)
    )
    to_row = jnp.where(valid[:, at] != 0, dst[:, at] - b * GH, -1)
    return rows_hot(line - b * GH, 3 * GH), rows_hot(to_row, GH)


def pick_both(rows_t, lists, odd, near, far):
    to_lower, to_upper = lists[0:1, :], lists[1:2, :]
    wanted = jnp.concatenate(
        [jnp.where(odd, to_lower, to_upper), jnp.where(odd, to_upper, to_lower)], axis=1
    )
    picked = dot(rows_t[...], rows_hot(wanted, rows_t.shape[1])).astype(BF)
    near[0 : picked.shape[0], :] = picked[:, :GH]
    far[0 : picked.shape[0], :] = picked[:, GH:]


def inner_kernel(layer, rows_t, weights, src, dst, valid, out, first, both, last, ends, sums):
    row_count = rows_t.shape[1]
    blocks = row_count // GH
    width = src.shape[1] // blocks
    first[...], both[...], last[...] = layer_weights([weights[layer, i] for i in range(6)])
    ends[...] = dot(first[...], rows_t[...]).astype(BF)

    def halves(b):
        return edge_halves(
            ends[0:128, (b - 1) * GH : (b + 2) * GH],
            ends[128:256, b * GH : (b + 1) * GH],
            *local_edges(b, row_count, src, dst, valid, width),
        )

    edge_sums(1, blocks - 1, halves, sums)
    step = (row_count - 2 * GH) // 2
    ranges = [slice(start, start + step) for start in (GH, GH + step)]
    pieces = [(rows_t[:, at], sums[:, at]) for at in ranges]
    for at, new in zip(ranges, node_updates(pieces, both[...], last[...])):
        out[:, at] = new


def by_side(place, near, far):
    odd = place[1] % 2 == 1
    return jnp.where(odd, near, far), jnp.where(odd, far, near)


def ghost_rows(place, before, after):
    nothing = jnp.zeros_like(before)
    return jnp.where(place[2] == 0, nothing, before), jnp.where(place[3] == 0, nothing, after)


def end_blocks(place, rows_t, ghosts, first, both, last, src, dst, valid):
    row_count = rows_t.shape[1]
    blocks = row_count // GH
    width = src.shape[1] // blocks
    before, after = ghost_rows(place, *ghosts)
    head, tail = rows_t[:, 0 : 2 * GH], rows_t[:, row_count - 2 * GH :]
    line = jnp.concatenate([before, head, tail, after], axis=1)
    ends = dot(first[...], line).astype(BF)
    halves = [
        edge_halves(
            ends[0:128, at : at + 3 * GH],
            ends[128:256, at + own : at + own + GH],
            *local_edges(b, row_count, src, dst, valid, width),
        )
        for b, at, own in ((0, 0, GH), (blocks - 1, 3 * GH, GH))
    ]
    own = jnp.concatenate([head[:, :GH], tail[:, GH:]], axis=1)
    sums = jnp.concatenate([edge_sum(*half) for half in halves], axis=1)
    return node_updates([(own, sums)], both[...], last[...])[0]


def whole_layer(inner, new, out):
    count = out.shape[1]
    out[:, GH : count - GH] = inner[:, GH : count - GH]
    out[:, 0:GH] = new[:, :GH]
    out[:, count - GH :] = new[:, GH:]


def ends_pick_kernel(place, inner, *refs):
    lists, cluster, facts, slot_row, out, near, far, more = refs[-8:]
    slots = dot(slot_row[...], rows_hot(cluster[...], 128)).astype(BF)
    ghosts = [rows.T for rows in by_side(place, refs[1][...], refs[2][...])]
    whole_layer(inner, end_blocks(place, refs[0], ghosts, *refs[3:-8]), out)
    more[0:128, :] = out[...]
    more[128:144, :] = slots
    pick_both(more, lists, place[1] % 2 == 1, near, far)
    near[144:208, :] = facts[0:64, :]
    far[144:208, :] = facts[0:64, :]


def ends_pool_kernel(place, inner, *refs):
    cluster, slot_pick, facts, out, parcel = refs[-5:]
    ghosts = by_side(place, refs[2][0:128, :], refs[1][0:128, :])
    whole_layer(inner, end_blocks(place, refs[0], ghosts, *refs[3:-5]), out)
    member = rows_hot(cluster[...], 128)
    partial = dot(out[...], member, NT).T.astype(BF)
    ids = by_side(place, refs[2][144:208, :], refs[1][144:208, :])
    lane = iota(ids[0].shape, 1)
    moved = [pltpu.roll(ids[side].astype(F32), CAP * (3 + side), 1) for side in (0, 1)]
    moved = [jnp.where(lane // CAP == 3 + side, moved[side], 0.0) for side in (0, 1)]
    added = moved[0] + moved[1]
    known = jnp.concatenate([added, jnp.zeros_like(added)], axis=0) + facts[...].astype(F32)
    parcel[...] = dot(
        slot_pick[...], jnp.concatenate([partial, known.astype(BF)], axis=0)
    ).astype(BF)


def turn_kernel(nodes, rows_t):
    rows_t[...] = nodes[...].T


def pick_kernel(place, rows_t, lists, near, far, meta_pick, spread):
    pick_both(rows_t, lists, place[1] % 2 == 1, near, far)
    count, total = meta_pick.shape
    owners = count // 3
    wide, pick = iota((count, total), 1), iota((count, total), 0)
    meta_pick[...] = hot(wide == SLOTS * (pick % owners) + 3 * CAP + pick // owners)
    spread[...] = hot((wide // SLOTS == pick % owners) & (wide % SLOTS // CAP == pick // owners))


def prepare_kernel(cluster, owner, coarse_row, ghosts, slot_pick, facts, slot_of, slot_row_out):
    member = rows_hot(cluster[...], 128)
    counts = jnp.sum(member.astype(F32), axis=1, keepdims=True)
    owner_row = owner[...].astype(F32)
    by_row, by_lane = column(owner_row), jnp.broadcast_to(owner_row, (128, 128))
    sub, lane = iota((128, 128), 0), iota((128, 128), 1)
    same = by_row == by_lane
    place_col = jnp.sum(jnp.where(same & (lane < sub), 1.0, 0.0), axis=1, keepdims=True)
    place_row = jnp.sum(jnp.where(same & (sub < lane), 1.0, 0.0), axis=0, keepdims=True)
    slot_row = owner_row * CAP + place_row
    owners = slot_pick.shape[0] // SLOTS
    slot_row_out[...] = jnp.broadcast_to(slot_row, slot_row_out.shape).astype(BF)
    row = iota((owners * SLOTS, 128), 0)
    to, at = row // SLOTS, row % SLOTS
    label = jnp.where(
        at < CAP,
        CAP * to + at,
        jnp.where(
            at < 2 * CAP,
            CAP * (to - 1) + at - CAP,
            jnp.where(at < 3 * CAP, CAP * (to + 1) + at - 2 * CAP, -1),
        ),
    )
    slot_pick[:, 0:128] = hot(label.astype(F32) == slot_row)
    back_row = iota(slot_of.shape, 0)
    back_to = over_back(back_row)
    back_at = back_row - BACK * back_to
    slot_of[...] = hot(
        jnp.where(back_at < CAP, CAP * back_to + back_at, -1).astype(F32) == slot_row
    )
    fact = jnp.where(
        at == 3 * CAP,
        to,
        jnp.where(
            at == 3 * CAP + 1,
            to - 1,
            jnp.where(at == 3 * CAP + 2, to + 1, jnp.where(at == 3 * CAP + 3, 127, -1)),
        ),
    )
    slot_pick[:, 128:256] = hot(fact == iota(fact.shape, 1))
    high = jnp.floor(counts / 16.0)
    low = counts - 16.0 * high
    lanes = lane.astype(F32)
    values = (
        jnp.where(lanes == place_col, column(coarse_row[...]), 0.0)
        + jnp.where(lanes == place_col + CAP, high, 0.0)
        + jnp.where(lanes == place_col + 2 * CAP, low, 0.0)
    ).astype(BF)
    meta = dot(hot(by_lane == sub.astype(F32)), values)
    each = ghosts.shape[2]
    listed = jnp.concatenate(
        [ghosts[0, 0:1], ghosts[0, 1:2], jnp.zeros((1, 128 - 2 * each), I32)], axis=1
    ).astype(F32)
    facts[...] = jnp.where(sub == 127, listed, meta).astype(BF)


def received_kernel(place, got, meta_pick, spread, part, own_metas):
    total = got.shape[0]
    owners = total // SLOTS
    here = place[0]
    metas = dot(meta_pick[...], got[...]).astype(BF)
    own_metas[...] = metas[0:owners]
    facts = dot(metas, spread[...], TN)[0:16]
    lane = iota((1, total), 1)
    turn = iota((16, total), 0) - iota((16, total), 1) % CAP

    def fact(number):
        return jnp.sum(jnp.where(turn == CAP * number, facts, 0.0), axis=0, keepdims=True)

    group = lane % SLOTS // CAP
    key = jnp.where(group < 3, fact(0) + (128 * group).astype(F32), -1.0)
    below = got[pl.ds(pl.multiple_of(jnp.maximum(here - 1, 0) * SLOTS, SLOTS), SLOTS), :]
    above = got[pl.ds(pl.multiple_of(jnp.minimum(here + 1, owners - 1) * SLOTS, SLOTS), SLOTS), :]
    below = column(below.astype(F32)[SLOTS - 1 : SLOTS, :])[16:32]
    above = column(above.astype(F32)[SLOTS - 1 : SLOTS, :])[0:16]
    label = jnp.concatenate(
        [
            iota((128, 128), 0, F32),
            jnp.where(here > 0, below + 128.0, -7.0),
            jnp.where(here < owners - 1, above + 256.0, -7.0),
            jnp.full((96, 128), -7.0, F32),
        ],
        axis=0,
    )
    label = jnp.concatenate([label] * (total // 128), axis=1)
    table = hot(label == key)
    part[0:160, :] = dot(table[0:160], got[...]).astype(BF)
    counted = dot(
        jnp.concatenate([fact(1), fact(2), jnp.zeros((6, total), F32)], axis=0).astype(BF),
        table,
        NT,
    )
    count = counted[0:1] * 16.0 + counted[1:2]
    third = jnp.floor(count / 65536.0)
    second = jnp.floor((count - 65536.0 * third) / 256.0)
    first = count - 65536.0 * third - 256.0 * second
    digits = [first, second, third]
    part[160:176, :] = jnp.concatenate(
        [d[:, 0:128] for d in digits]
        + [d[:, 128:256] for d in digits]
        + [jnp.zeros((10, 128), F32)],
        axis=0,
    ).astype(BF)


def ready_kernel(own_metas, weights, src, dst, near, far, *outs):
    back, first, both, last, from_hot, to_hot, first3, both3, last3 = outs
    owners = own_metas.shape[0]
    total = BACK * owners
    ids = dot(hot(over_back(iota((total, owners), 0)) == iota((total, owners), 1)), own_metas[...])
    row = iota((total, 128), 0)
    at = row - BACK * over_back(row)
    lanes = iota((total, 128), 1)
    wanted = jnp.where(at < CAP, at, at + 2 * CAP)
    named = jnp.sum(jnp.where(lanes == wanted, ids, 0.0), axis=1, keepdims=True)
    back[...] = hot(lanes.astype(F32) == named)
    first[...], both[...], last[...] = layer_weights([weights[2, i] for i in range(6)])
    first3[...], both3[...], last3[...] = layer_weights([weights[3, i] for i in range(6)])
    from_hot[...] = rows_hot(src[...], 160)
    to_hot[...] = rows_hot(dst[...], 128)


def coarse_kernel(own, other1, other2, other3, back, first, both, last, from_hot, to_hot, out, reply):
    whole = (own[...].astype(F32) + other1[...].astype(F32)) + (
        other2[...].astype(F32) + other3[...].astype(F32)
    )

    def counts(at):
        row = whole[at : at + 1] + 256.0 * whole[at + 1 : at + 2] + 65536.0 * whole[at + 2 : at + 3]
        return jnp.maximum(row, 1.0)

    rows_t = (whole[0:128].T / counts(160)).astype(BF)
    ghosts = jnp.concatenate([whole[128:160], jnp.zeros((96, 128), F32)], axis=0)
    ghosts_t = (ghosts.T / counts(163)).astype(BF)
    ends = dot(first[...], jnp.concatenate([rows_t, ghosts_t], axis=1)).astype(BF)
    half = dot(ends[0:128, 0:160], from_hot[...]) + dot(ends[128:256, 0:128], to_hot[...])
    sums = dot(half_silu(half).astype(BF), to_hot[...], NT).astype(BF)
    new = node_updates([(rows_t, sums)], both[...], last[...])[0].T
    out[...] = new
    reply[...] = dot(back[...], new).astype(BF)


def final_kernel(
    place,
    rows_t,
    reply,
    slot_of,
    cluster,
    early_far,
    early_near,
    from_far,
    from_near,
    first,
    both,
    last,
    src,
    dst,
    valid,
    out,
    line,
    ends,
    sums,
    done,
    sems,
):
    row_count = rows_t.shape[1]
    blocks = row_count // GH
    width = src.shape[1] // blocks
    tables = [slot_of[...]]
    for at, slots in enumerate(by_side(place, early_near[128:144, :], early_far[128:144, :])):
        slot = slots.astype(F32).astype(I32)[0:1]
        tables.append(rows_hot(slot // CAP * BACK + slot % CAP + CAP * (at + 1), reply.shape[0]))
    coarse = dot(reply[...], jnp.concatenate(tables, axis=1), TN)
    member = rows_hot(cluster[...], 128)
    before, after = by_side(place, from_near[...], from_far[...])
    before = (before.astype(F32) + coarse[:, 128:256]).astype(BF)
    after = (after.astype(F32) + coarse[:, 256:384]).astype(BF)
    line[:, 0:GH], line[:, GH + row_count :] = ghost_rows(place, before, after)
    line[:, GH : GH + row_count] = (
        rows_t[...].astype(F32) + dot(coarse[:, 0:128].astype(BF), member)
    ).astype(BF)
    ends[...] = dot(first[...], line[...]).astype(BF)
    parts = sems.shape[0]
    step = row_count // parts
    copies = []

    def halves(b):
        return edge_halves(
            ends[0:128, b * GH : (b + 3) * GH],
            ends[128:256, (b + 1) * GH : (b + 2) * GH],
            *local_edges(b, row_count, src, dst, valid, width),
        )

    edge_sums(0, blocks, halves, sums)
    starts = [part * step for part in range(parts)]
    pieces = [
        (line[:, GH + start : GH + start + step], sums[:, start : start + step]) for start in starts
    ]
    for part, new in enumerate(node_updates(pieces, both[...], last[...])):
        start = starts[part]
        at = pl.ds(start, step)
        done[at, :] = new.T
        copies.append(pltpu.make_async_copy(done.at[at, :], out.at[at, :], sems.at[part]))
        copies[-1].start()
    for copy in copies:
        copy.wait()


def run(kernel, outs, args, scalars=0, layer=None, scratch=(), flops=0, out_space=pltpu.VMEM, name=None):
    specs = []
    for i in range(len(args)):
        specs.append(pl.BlockSpec(memory_space=pltpu.SMEM if i < scalars else pltpu.VMEM))
    return pl.pallas_call(
        kernel if layer is None else functools.partial(kernel, layer),
        out_shape=[jax.ShapeDtypeStruct(shape, BF) for shape in outs],
        in_specs=specs,
        out_specs=[pl.BlockSpec(memory_space=out_space) for _ in outs],
        scratch_shapes=scratch,
        compiler_params=pltpu.CompilerParams(vmem_limit_bytes=VMEM_LIMIT),
        cost_estimate=pl.CostEstimate(flops=flops, bytes_accessed=1 << 20, transcendentals=0),
        name=name,
    )(*args)


def on_device(
    nodes,
    weights,
    edge_src,
    edge_dst,
    edge_valid,
    ghost_list,
    cluster_of,
    owner,
    coarse_row,
    coarse_src,
    coarse_dst,
    coarse_ghosts,
):
    count, width = nodes.shape
    doms, subs = lax.axis_size("dom"), lax.axis_size("sub")
    dom, sub = lax.axis_index("dom"), lax.axis_index("sub")
    chain = doms * subs
    index = dom * subs + sub
    place = jnp.stack([dom, sub, index, chain - 1 - index]).astype(I32)
    lists = ghost_list[0]
    edges = (edge_src, edge_dst, edge_valid)
    ghost = (width, GH)
    rows_t = (width, count)
    forms = [(2 * width, width), (width, 2 * width), (width, width)]
    near_pairs = [(i, i ^ 1) for i in range(chain)]
    far_pairs = [(i, (i + 1 if i % 2 else i - 1) % chain) for i in range(chain)]

    def swap(near, far):
        from_far = lax.ppermute(far, ("dom", "sub"), far_pairs)
        from_near = lax.ppermute(near, ("dom", "sub"), near_pairs)
        return from_far, from_near

    def inner(states, layer):
        out, *weights_now = run(
            inner_kernel,
            [rows_t] + forms,
            (states, weights) + edges,
            layer=layer,
            scratch=[pltpu.VMEM((2 * width, count), BF), pltpu.VMEM(rows_t, BF)],
            flops=4 * 10**9,
            name="inner",
        )
        return out, tuple(weights_now)

    wanted = lists.reshape(-1, 1) == jnp.arange(count, dtype=I32)[None, :]
    picked = dot(wanted.astype(BF), nodes).astype(BF)
    odd = sub % 2 == 1
    ghosts = swap(
        jnp.where(odd, picked[:GH], picked[GH:]), jnp.where(odd, picked[GH:], picked[:GH])
    )
    (states,) = run(turn_kernel, [rows_t], (nodes,), flops=3 * 10**8, name="turn")
    slot_pick, facts, slot_of, slot_row = run(
        prepare_kernel,
        [(doms * SLOTS, 256), (128, 128), (doms * BACK, 128), (16, 128)],
        (cluster_of, owner.reshape(1, -1), coarse_row, coarse_ghosts),
        flops=10**9,
        name="prepare",
    )
    middle, now = inner(states, 0)
    early = (GH + 16 + doms, GH)
    states, near, far = run(
        ends_pick_kernel,
        [rows_t, early, early],
        (place, middle, states) + ghosts[::-1] + now + edges + (lists, cluster_of, facts, slot_row),
        scalars=1,
        scratch=[pltpu.VMEM((width + 16, count), BF)],
        flops=10**9,
        name="ends_pick",
    )
    early = swap(near, far)
    middle, now = inner(states, 1)
    states, parcel = run(
        ends_pool_kernel,
        [rows_t, (doms * SLOTS, width)],
        (place, middle, states) + early + now + edges + (cluster_of, slot_pick, facts),
        scalars=1,
        flops=10**9,
        name="ends_pool",
    )
    near, far, meta_pick, spread = run(
        pick_kernel,
        [ghost, ghost] + [(3 * doms, doms * SLOTS)] * 2,
        (place, states, lists),
        scalars=1,
        flops=10**9,
        name="pick",
    )
    ghosts = swap(near, far)

    def exchange(rows):
        shape = rows.shape
        rows = rows.reshape(doms, shape[0] // doms, width)
        rows = lax.all_to_all(rows, "dom", split_axis=0, concat_axis=0, tiled=True)
        return rows.reshape(shape)

    part, own_metas = run(
        received_kernel,
        [(176, width), (doms, width)],
        (place, exchange(parcel), meta_pick, spread),
        scalars=1,
        flops=10**9,
        name="received",
    )
    others = [lax.ppermute(part, "sub", [(i, i ^ k) for i in range(subs)]) for k in (1, 2, 3)]
    back, *ready = run(
        ready_kernel,
        [(doms * BACK, width)]
        + forms
        + [(160, coarse_src.shape[1]), (128, coarse_src.shape[1])]
        + forms,
        (own_metas, weights, coarse_src, coarse_dst) + ghosts,
        flops=10**9,
        name="ready",
    )
    coarse, reply = run(
        coarse_kernel,
        [(128, width), (doms * BACK, width)],
        (part, *others, back, *ready[:5]),
        flops=10**9,
        name="coarse",
    )
    (last,) = run(
        final_kernel,
        [nodes.shape],
        (place, states, exchange(reply), slot_of, cluster_of) + early + ghosts + tuple(ready[5:8]) + edges,
        scalars=1,
        scratch=[
            pltpu.VMEM((width, count + 2 * GH), BF),
            pltpu.VMEM((2 * width, count + 2 * GH), BF),
            pltpu.VMEM(rows_t, BF),
            pltpu.VMEM(nodes.shape, BF),
            pltpu.SemaphoreType.DMA((FINAL_PARTS,)),
        ],
        out_space=pl.ANY,
        flops=5 * 10**9,
        name="final",
    )
    return (last, coarse)


def solution(mesh):
    placed = (
        P(("dom", "sub"), None),
        P(),
        P(("dom", "sub"), None),
        P(("dom", "sub"), None),
        P(("dom", "sub"), None),
        P(("dom", "sub"), None, None),
        P(("dom", "sub"), None),
        P(("dom", "sub"), None, None),
        P(("dom", "sub"), None),
        P("dom", None),
        P("dom", None),
        P("dom", None, None),
    )
    return jax.shard_map(
        on_device,
        mesh=mesh,
        in_specs=placed,
        out_specs=(P(("dom", "sub"), None), P("dom", None)),
        check_vma=False,
    )
```

```python
import functools

import jax
import jax.numpy as jnp
from jax import lax
from jax.experimental import pallas as pl
from jax.experimental.pallas import tpu as pltpu
from jax.sharding import PartitionSpec as P

BF = jnp.bfloat16
F32 = jnp.float32
I32 = jnp.int32
I16 = jnp.int16
NN = (((1,), (0,)), ((), ()))
NT = (((1,), (1,)), ((), ()))
TN = (((0,), (0,)), ((), ()))

GH = 128
CAP = 4
SLOTS = 16
BACK = 3 * CAP
VMEM_LIMIT = 28 << 20
FINAL_PARTS = 2


def dot(left, right, dims=NN):
    return lax.dot_general(left, right, dims, preferred_element_type=F32)


def iota(shape, dim, dtype=I32):
    return lax.broadcasted_iota(I32, shape, dim).astype(dtype)


def hot(mask):
    return jnp.where(mask, 1.0, 0.0).astype(BF)


def column(row):
    return jnp.broadcast_to(row.astype(F32), (128, 128)).T


def half_silu(half):
    return half * (1.0 + jnp.tanh(half))


def rows_hot(index_row, count):
    table = lax.broadcasted_iota(I16, (count, index_row.shape[1]), 0)
    return jnp.where(table == index_row.astype(I16), BF(1), BF(0))


def over_back(row):
    return (row * (65536 // BACK + 1)) >> 16


def edge_halves(source_t, target_t, from_hot, to_hot):
    table = jnp.concatenate([source_t, target_t], axis=1)
    return dot(table, jnp.concatenate([from_hot, to_hot], axis=0)), to_hot


def edge_sum(half, to_hot):
    return dot(half_silu(half).astype(BF), to_hot, NT).astype(BF)


def edge_sums(first, last, halves, sums):
    ahead = halves(first)
    for b in range(first, last):
        now, ahead = ahead, halves(b + 1) if b + 1 < last else None
        sums[:, b * GH : (b + 1) * GH] = edge_sum(*now)


def layer_weights(w):
    first = jnp.concatenate([w[0].astype(F32).T, w[1].astype(F32).T], axis=0) * 0.5
    both = jnp.concatenate([w[3].astype(F32).T, dot(w[2], w[4]).T], axis=1) * 0.5
    last = w[5].astype(F32)
    last = last - jnp.mean(last, axis=1, keepdims=True)
    return first.astype(BF), both.astype(BF), last.T.astype(BF)


def node_updates(pieces, both, last):
    halves = [dot(both, jnp.concatenate(piece, axis=0)) for piece in pieces]
    centred = [dot(last, half_silu(half).astype(BF)) for half in halves]
    new = []
    for (rows_t, _), piece in zip(pieces, centred):
        spread = jnp.mean(piece * piece, axis=0, keepdims=True)
        new.append((rows_t.astype(F32) + piece * lax.rsqrt(spread + 1e-5)).astype(BF))
    return new


def local_edges(b, row_count, src, dst, valid, width):
    at = pl.ds(b * width, width)
    edge = src[:, at]
    line = jnp.where(
        edge < row_count, edge + GH, jnp.where(edge < row_count + GH, edge - row_count, edge)
    )
    to_row = jnp.where(valid[:, at] != 0, dst[:, at] - b * GH, -1)
    return rows_hot(line - b * GH, 3 * GH), rows_hot(to_row, GH)


def wanted_rows(place, lists):
    odd = place[1] % 2 == 1
    to_lower, to_upper = lists[0:1, :], lists[1:2, :]
    return jnp.concatenate(
        [jnp.where(odd, to_lower, to_upper), jnp.where(odd, to_upper, to_lower)], axis=1
    )


def inner_kernel(layer, rows_t, weights, src, dst, valid, out, first, both, last, ends, sums):
    row_count = rows_t.shape[1]
    blocks = row_count // GH
    width = src.shape[1] // blocks
    first[...], both[...], last[...] = layer_weights([weights[layer, i] for i in range(6)])
    ends[...] = dot(first[...], rows_t[...]).astype(BF)

    def halves(b):
        return edge_halves(
            ends[0:128, (b - 1) * GH : (b + 2) * GH],
            ends[128:256, b * GH : (b + 1) * GH],
            *local_edges(b, row_count, src, dst, valid, width),
        )

    edge_sums(1, blocks - 1, halves, sums)
    step = (row_count - 2 * GH) // 2
    ranges = [slice(start, start + step) for start in (GH, GH + step)]
    pieces = [(rows_t[:, at], sums[:, at]) for at in ranges]
    for at, new in zip(ranges, node_updates(pieces, both[...], last[...])):
        out[:, at] = new


def inner_pick_kernel(layer, place, lists, rows_t, weights, src, dst, valid, out, *refs):
    first, both, last, picked, ends, sums = refs
    inner_kernel(layer, rows_t, weights, src, dst, valid, out, first, both, last, ends, sums)
    count = out.shape[1]
    table = rows_hot(wanted_rows(place, lists) - GH, count - 2 * GH)
    picked[...] = dot(out[:, GH : count - GH], table).astype(BF)


def inner_pool_kernel(layer, cluster, rows_t, weights, src, dst, valid, out, *refs):
    first, both, last, pooled, ends, sums = refs
    inner_kernel(layer, rows_t, weights, src, dst, valid, out, first, both, last, ends, sums)
    count = out.shape[1]
    member = rows_hot(cluster[:, GH : count - GH], 128)
    pooled[...] = dot(out[:, GH : count - GH], member, NT)


def by_side(place, near, far):
    odd = place[1] % 2 == 1
    return jnp.where(odd, near, far), jnp.where(odd, far, near)


def ghost_rows(place, before, after):
    nothing = jnp.zeros_like(before)
    return jnp.where(place[2] == 0, nothing, before), jnp.where(place[3] == 0, nothing, after)


def end_blocks(place, rows_t, ghosts, first, both, last, src, dst, valid):
    row_count = rows_t.shape[1]
    blocks = row_count // GH
    width = src.shape[1] // blocks
    before, after = ghost_rows(place, *ghosts)
    head, tail = rows_t[:, 0 : 2 * GH], rows_t[:, row_count - 2 * GH :]
    line = jnp.concatenate([before, head, tail, after], axis=1)
    ends = dot(first[...], line).astype(BF)
    halves = [
        edge_halves(
            ends[0:128, at : at + 3 * GH],
            ends[128:256, at + own : at + own + GH],
            *local_edges(b, row_count, src, dst, valid, width),
        )
        for b, at, own in ((0, 0, GH), (blocks - 1, 3 * GH, GH))
    ]
    own = jnp.concatenate([head[:, :GH], tail[:, GH:]], axis=1)
    sums = jnp.concatenate([edge_sum(*half) for half in halves], axis=1)
    return node_updates([(own, sums)], both[...], last[...])[0]


def whole_layer(inner, new, out):
    count = out.shape[1]
    out[:, GH : count - GH] = inner[:, GH : count - GH]
    out[:, 0:GH] = new[:, :GH]
    out[:, count - GH :] = new[:, GH:]


def ends_pick_kernel(place, inner, *refs):
    lists, picked, slots, facts, out, near, far = refs[-7:]
    ghosts = [rows.T for rows in by_side(place, refs[1][...], refs[2][...])]
    new = end_blocks(place, refs[0], ghosts, *refs[3:-7])
    wanted = wanted_rows(place, lists)
    table = [rows_hot(wanted, GH), rows_hot(wanted - (out.shape[1] - GH), GH)]
    rows = picked[...].astype(F32) + dot(new, jnp.concatenate(table, axis=0))
    whole_layer(inner, new, out)
    for side, ref in enumerate((near, far)):
        ref[0:128, :] = rows[:, side * GH : (side + 1) * GH].astype(BF)
        ref[128:144, :] = slots[:, side * GH : (side + 1) * GH]
        ref[144:208, :] = facts[0:64, :]


def ends_pool_kernel(place, inner, *refs):
    cluster, pooled, slot_pick, facts, out, parcel = refs[-6:]
    ghosts = by_side(place, refs[2][0:128, :], refs[1][0:128, :])
    new = end_blocks(place, refs[0], ghosts, *refs[3:-6])
    whole_layer(inner, new, out)
    count = out.shape[1]
    named = jnp.concatenate([cluster[:, 0:GH], cluster[:, count - GH :]], axis=1)
    partial = (pooled[...] + dot(new, rows_hot(named, 128), NT)).T.astype(BF)
    ids = by_side(place, refs[2][144:208, :], refs[1][144:208, :])
    lane = iota(ids[0].shape, 1)
    moved = [pltpu.roll(ids[side].astype(F32), CAP * (3 + side), 1) for side in (0, 1)]
    moved = [jnp.where(lane // CAP == 3 + side, moved[side], 0.0) for side in (0, 1)]
    added = moved[0] + moved[1]
    known = jnp.concatenate([added, jnp.zeros_like(added)], axis=0) + facts[...].astype(F32)
    parcel[...] = dot(
        slot_pick[...], jnp.concatenate([partial, known.astype(BF)], axis=0)
    ).astype(BF)


def turn_kernel(nodes, rows_t):
    rows_t[...] = nodes[...].T


def pick_kernel(place, rows_t, lists, near, far, meta_pick, spread):
    picked = dot(rows_t[...], rows_hot(wanted_rows(place, lists), rows_t.shape[1])).astype(BF)
    near[...], far[...] = picked[:, :GH], picked[:, GH:]
    count, total = meta_pick.shape
    owners = count // 3
    wide, pick = iota((count, total), 1), iota((count, total), 0)
    meta_pick[...] = hot(wide == SLOTS * (pick % owners) + 3 * CAP + pick // owners)
    spread[...] = hot((wide // SLOTS == pick % owners) & (wide % SLOTS // CAP == pick // owners))


def prepare_kernel(
    place, lists, cluster, owner, coarse_row, ghosts, slot_pick, facts, slot_of, slots
):
    member = rows_hot(cluster[...], 128)
    counts = jnp.sum(member.astype(F32), axis=1, keepdims=True)
    owner_row = owner[...].astype(F32)
    by_row, by_lane = column(owner_row), jnp.broadcast_to(owner_row, (128, 128))
    sub, lane = iota((128, 128), 0), iota((128, 128), 1)
    same = by_row == by_lane
    place_col = jnp.sum(jnp.where(same & (lane < sub), 1.0, 0.0), axis=1, keepdims=True)
    place_row = jnp.sum(jnp.where(same & (sub < lane), 1.0, 0.0), axis=0, keepdims=True)
    slot_row = owner_row * CAP + place_row
    owners = slot_pick.shape[0] // SLOTS
    every = dot(jnp.broadcast_to(slot_row, (16, 128)).astype(BF), member).astype(BF)
    slots[...] = dot(every, rows_hot(wanted_rows(place, lists), cluster.shape[1])).astype(BF)
    row = iota((owners * SLOTS, 128), 0)
    to, at = row // SLOTS, row % SLOTS
    label = jnp.where(
        at < CAP,
        CAP * to + at,
        jnp.where(
            at < 2 * CAP,
            CAP * (to - 1) + at - CAP,
            jnp.where(at < 3 * CAP, CAP * (to + 1) + at - 2 * CAP, -1),
        ),
    )
    slot_pick[:, 0:128] = hot(label.astype(F32) == slot_row)
    back_row = iota(slot_of.shape, 0)
    back_to = over_back(back_row)
    back_at = back_row - BACK * back_to
    slot_of[...] = hot(
        jnp.where(back_at < CAP, CAP * back_to + back_at, -1).astype(F32) == slot_row
    )
    fact = jnp.where(
        at == 3 * CAP,
        to,
        jnp.where(
            at == 3 * CAP + 1,
            to - 1,
            jnp.where(at == 3 * CAP + 2, to + 1, jnp.where(at == 3 * CAP + 3, 127, -1)),
        ),
    )
    slot_pick[:, 128:256] = hot(fact == iota(fact.shape, 1))
    high = jnp.floor(counts / 16.0)
    low = counts - 16.0 * high
    lanes = lane.astype(F32)
    values = (
        jnp.where(lanes == place_col, column(coarse_row[...]), 0.0)
        + jnp.where(lanes == place_col + CAP, high, 0.0)
        + jnp.where(lanes == place_col + 2 * CAP, low, 0.0)
    ).astype(BF)
    meta = dot(hot(by_lane == sub.astype(F32)), values)
    each = ghosts.shape[2]
    listed = jnp.concatenate(
        [ghosts[0, 0:1], ghosts[0, 1:2], jnp.zeros((1, 128 - 2 * each), I32)], axis=1
    ).astype(F32)
    facts[...] = jnp.where(sub == 127, listed, meta).astype(BF)


def received_kernel(place, got, meta_pick, spread, part, own_metas):
    total = got.shape[0]
    owners = total // SLOTS
    here = place[0]
    metas = dot(meta_pick[...], got[...]).astype(BF)
    own_metas[...] = metas[0:owners]
    facts = dot(metas, spread[...], TN)[0:16]
    lane = iota((1, total), 1)
    turn = iota((16, total), 0) - iota((16, total), 1) % CAP

    def fact(number):
        return jnp.sum(jnp.where(turn == CAP * number, facts, 0.0), axis=0, keepdims=True)

    group = lane % SLOTS // CAP
    key = jnp.where(group < 3, fact(0) + (128 * group).astype(F32), -1.0)
    below = got[pl.ds(pl.multiple_of(jnp.maximum(here - 1, 0) * SLOTS, SLOTS), SLOTS), :]
    above = got[pl.ds(pl.multiple_of(jnp.minimum(here + 1, owners - 1) * SLOTS, SLOTS), SLOTS), :]
    below = column(below.astype(F32)[SLOTS - 1 : SLOTS, :])[16:32]
    above = column(above.astype(F32)[SLOTS - 1 : SLOTS, :])[0:16]
    label = jnp.concatenate(
        [
            iota((128, 128), 0, F32),
            jnp.where(here > 0, below + 128.0, -7.0),
            jnp.where(here < owners - 1, above + 256.0, -7.0),
            jnp.full((96, 128), -7.0, F32),
        ],
        axis=0,
    )
    label = jnp.concatenate([label] * (total // 128), axis=1)
    table = hot(label == key)
    part[0:160, :] = dot(table[0:160], got[...]).astype(BF)
    counted = dot(
        jnp.concatenate([fact(1), fact(2), jnp.zeros((6, total), F32)], axis=0).astype(BF),
        table,
        NT,
    )
    count = counted[0:1] * 16.0 + counted[1:2]
    third = jnp.floor(count / 65536.0)
    second = jnp.floor((count - 65536.0 * third) / 256.0)
    first = count - 65536.0 * third - 256.0 * second
    digits = [first, second, third]
    part[160:176, :] = jnp.concatenate(
        [d[:, 0:128] for d in digits]
        + [d[:, 128:256] for d in digits]
        + [jnp.zeros((10, 128), F32)],
        axis=0,
    ).astype(BF)


def ready_kernel(own_metas, weights, src, dst, near, far, *outs):
    back, first, both, last, from_hot, to_hot, first3, both3, last3 = outs
    owners = own_metas.shape[0]
    total = BACK * owners
    ids = dot(hot(over_back(iota((total, owners), 0)) == iota((total, owners), 1)), own_metas[...])
    row = iota((total, 128), 0)
    at = row - BACK * over_back(row)
    lanes = iota((total, 128), 1)
    wanted = jnp.where(at < CAP, at, at + 2 * CAP)
    named = jnp.sum(jnp.where(lanes == wanted, ids, 0.0), axis=1, keepdims=True)
    back[...] = hot(lanes.astype(F32) == named)
    first[...], both[...], last[...] = layer_weights([weights[2, i] for i in range(6)])
    first3[...], both3[...], last3[...] = layer_weights([weights[3, i] for i in range(6)])
    from_hot[...] = rows_hot(src[...], 160)
    to_hot[...] = rows_hot(dst[...], 128)


def coarse_kernel(own, other1, other2, other3, back, first, both, last, from_hot, to_hot, out, reply):
    whole = (own[...].astype(F32) + other1[...].astype(F32)) + (
        other2[...].astype(F32) + other3[...].astype(F32)
    )

    def counts(at):
        row = whole[at : at + 1] + 256.0 * whole[at + 1 : at + 2] + 65536.0 * whole[at + 2 : at + 3]
        return jnp.maximum(row, 1.0)

    rows_t = (whole[0:128].T / counts(160)).astype(BF)
    ghosts = jnp.concatenate([whole[128:160], jnp.zeros((96, 128), F32)], axis=0)
    ghosts_t = (ghosts.T / counts(163)).astype(BF)
    ends = dot(first[...], jnp.concatenate([rows_t, ghosts_t], axis=1)).astype(BF)
    half = dot(ends[0:128, 0:160], from_hot[...]) + dot(ends[128:256, 0:128], to_hot[...])
    sums = dot(half_silu(half).astype(BF), to_hot[...], NT).astype(BF)
    new = node_updates([(rows_t, sums)], both[...], last[...])[0].T
    out[...] = new
    reply[...] = dot(back[...], new).astype(BF)


def final_kernel(
    place,
    rows_t,
    reply,
    slot_of,
    cluster,
    early_far,
    early_near,
    from_far,
    from_near,
    first,
    both,
    last,
    src,
    dst,
    valid,
    out,
    line,
    ends,
    sums,
    done,
    sems,
):
    row_count = rows_t.shape[1]
    blocks = row_count // GH
    width = src.shape[1] // blocks
    tables = [slot_of[...]]
    for at, slots in enumerate(by_side(place, early_near[128:144, :], early_far[128:144, :])):
        slot = slots.astype(F32).astype(I32)[0:1]
        tables.append(rows_hot(slot // CAP * BACK + slot % CAP + CAP * (at + 1), reply.shape[0]))
    coarse = dot(reply[...], jnp.concatenate(tables, axis=1), TN)
    member = rows_hot(cluster[...], 128)
    before, after = by_side(place, from_near[...], from_far[...])
    before = (before.astype(F32) + coarse[:, 128:256]).astype(BF)
    after = (after.astype(F32) + coarse[:, 256:384]).astype(BF)
    line[:, 0:GH], line[:, GH + row_count :] = ghost_rows(place, before, after)
    line[:, GH : GH + row_count] = (
        rows_t[...].astype(F32) + dot(coarse[:, 0:128].astype(BF), member)
    ).astype(BF)
    ends[...] = dot(first[...], line[...]).astype(BF)
    parts = sems.shape[0]
    step = row_count // parts
    copies = []

    def halves(b):
        return edge_halves(
            ends[0:128, b * GH : (b + 3) * GH],
            ends[128:256, (b + 1) * GH : (b + 2) * GH],
            *local_edges(b, row_count, src, dst, valid, width),
        )

    edge_sums(0, blocks, halves, sums)
    starts = [part * step for part in range(parts)]
    pieces = [
        (line[:, GH + start : GH + start + step], sums[:, start : start + step]) for start in starts
    ]
    for part, new in enumerate(node_updates(pieces, both[...], last[...])):
        start = starts[part]
        at = pl.ds(start, step)
        done[at, :] = new.T
        copies.append(pltpu.make_async_copy(done.at[at, :], out.at[at, :], sems.at[part]))
        copies[-1].start()
    for copy in copies:
        copy.wait()


def run(kernel, outs, args, scalars=0, layer=None, scratch=(), flops=0, out_space=pltpu.VMEM, wide=None, name=None):
    specs = []
    for i in range(len(args)):
        specs.append(pl.BlockSpec(memory_space=pltpu.SMEM if i < scalars else pltpu.VMEM))
    return pl.pallas_call(
        kernel if layer is None else functools.partial(kernel, layer),
        out_shape=[
            jax.ShapeDtypeStruct(shape, F32 if i == wide else BF) for i, shape in enumerate(outs)
        ],
        in_specs=specs,
        out_specs=[pl.BlockSpec(memory_space=out_space) for _ in outs],
        scratch_shapes=scratch,
        compiler_params=pltpu.CompilerParams(vmem_limit_bytes=VMEM_LIMIT),
        cost_estimate=pl.CostEstimate(flops=flops, bytes_accessed=1 << 20, transcendentals=0),
        name=name,
    )(*args)


def on_device(
    nodes,
    weights,
    edge_src,
    edge_dst,
    edge_valid,
    ghost_list,
    cluster_of,
    owner,
    coarse_row,
    coarse_src,
    coarse_dst,
    coarse_ghosts,
):
    count, width = nodes.shape
    doms, subs = lax.axis_size("dom"), lax.axis_size("sub")
    dom, sub = lax.axis_index("dom"), lax.axis_index("sub")
    chain = doms * subs
    index = dom * subs + sub
    place = jnp.stack([dom, sub, index, chain - 1 - index]).astype(I32)
    lists = ghost_list[0]
    edges = (edge_src, edge_dst, edge_valid)
    ghost = (width, GH)
    rows_t = (width, count)
    forms = [(2 * width, width), (width, 2 * width), (width, width)]
    near_pairs = [(i, i ^ 1) for i in range(chain)]
    far_pairs = [(i, (i + 1 if i % 2 else i - 1) % chain) for i in range(chain)]

    def swap(near, far):
        from_far = lax.ppermute(far, ("dom", "sub"), far_pairs)
        from_near = lax.ppermute(near, ("dom", "sub"), near_pairs)
        return from_far, from_near

    def inner(kernel, before, states, layer, more, **options):
        out, first, both, last, extra = run(
            kernel,
            [rows_t] + forms + [more],
            before + (states, weights) + edges,
            layer=layer,
            scratch=[pltpu.VMEM((2 * width, count), BF), pltpu.VMEM(rows_t, BF)],
            flops=4 * 10**9,
            **options,
        )
        return out, (first, both, last), extra

    wanted = lists.reshape(-1, 1) == jnp.arange(count, dtype=I32)[None, :]
    picked = dot(wanted.astype(BF), nodes).astype(BF)
    odd = sub % 2 == 1
    ghosts = swap(
        jnp.where(odd, picked[:GH], picked[GH:]), jnp.where(odd, picked[GH:], picked[:GH])
    )
    (states,) = run(turn_kernel, [rows_t], (nodes,), flops=3 * 10**8, name="turn")
    slot_pick, facts, slot_of, slots = run(
        prepare_kernel,
        [(doms * SLOTS, 256), (128, 128), (doms * BACK, 128), (16, 2 * GH)],
        (place, lists, cluster_of, owner.reshape(1, -1), coarse_row, coarse_ghosts),
        scalars=1,
        flops=10**9,
        name="prepare",
    )
    middle, now, picked = inner(
        inner_pick_kernel, (place, lists), states, 0, (width, 2 * GH), scalars=1, name="inner_pick"
    )
    early = (GH + 16 + doms, GH)
    states, near, far = run(
        ends_pick_kernel,
        [rows_t, early, early],
        (place, middle, states) + ghosts[::-1] + now + edges + (lists, picked, slots, facts),
        scalars=1,
        flops=10**9,
        name="ends_pick",
    )
    early = swap(near, far)
    middle, now, pooled = inner(
        inner_pool_kernel, (cluster_of,), states, 1, (width, 128), wide=4, name="inner_pool"
    )
    states, parcel = run(
        ends_pool_kernel,
        [rows_t, (doms * SLOTS, width)],
        (place, middle, states) + early + now + edges + (cluster_of, pooled, slot_pick, facts),
        scalars=1,
        flops=10**9,
        name="ends_pool",
    )
    near, far, meta_pick, spread = run(
        pick_kernel,
        [ghost, ghost] + [(3 * doms, doms * SLOTS)] * 2,
        (place, states, lists),
        scalars=1,
        flops=10**9,
        name="pick",
    )
    ghosts = swap(near, far)

    def exchange(rows):
        shape = rows.shape
        each = 4 if shape[0] // doms % 8 else 8
        rows = rows.reshape(-1, each, width)
        rows = lax.all_to_all(rows, "dom", split_axis=0, concat_axis=0, tiled=True)
        return rows.reshape(shape)

    part, own_metas = run(
        received_kernel,
        [(176, width), (doms, width)],
        (place, exchange(parcel), meta_pick, spread),
        scalars=1,
        flops=10**9,
        name="received",
    )
    others = [lax.ppermute(part, "sub", [(i, i ^ k) for i in range(subs)]) for k in (1, 2, 3)]
    back, *ready = run(
        ready_kernel,
        [(doms * BACK, width)]
        + forms
        + [(160, coarse_src.shape[1]), (128, coarse_src.shape[1])]
        + forms,
        (own_metas, weights, coarse_src, coarse_dst) + ghosts,
        flops=10**9,
        name="ready",
    )
    coarse, reply = run(
        coarse_kernel,
        [(128, width), (doms * BACK, width)],
        (part, *others, back, *ready[:5]),
        flops=10**9,
        name="coarse",
    )
    (last,) = run(
        final_kernel,
        [nodes.shape],
        (place, states, exchange(reply), slot_of, cluster_of) + early + ghosts + tuple(ready[5:8]) + edges,
        scalars=1,
        scratch=[
            pltpu.VMEM((width, count + 2 * GH), BF),
            pltpu.VMEM((2 * width, count + 2 * GH), BF),
            pltpu.VMEM(rows_t, BF),
            pltpu.VMEM(nodes.shape, BF),
            pltpu.SemaphoreType.DMA((FINAL_PARTS,)),
        ],
        out_space=pl.ANY,
        flops=5 * 10**9,
        name="final",
    )
    return (last, coarse)


def solution(mesh):
    placed = (
        P(("dom", "sub"), None),
        P(),
        P(("dom", "sub"), None),
        P(("dom", "sub"), None),
        P(("dom", "sub"), None),
        P(("dom", "sub"), None, None),
        P(("dom", "sub"), None),
        P(("dom", "sub"), None, None),
        P(("dom", "sub"), None),
        P("dom", None),
        P("dom", None),
        P("dom", None, None),
    )
    return jax.shard_map(
        on_device,
        mesh=mesh,
        in_specs=placed,
        out_specs=(P(("dom", "sub"), None), P("dom", None)),
        check_vma=False,
    )
```

```python
import functools

import jax
import jax.numpy as jnp
from jax import lax
from jax.experimental import pallas as pl
from jax.experimental.pallas import tpu as pltpu
from jax.sharding import PartitionSpec as P

BF = jnp.bfloat16
F32 = jnp.float32
I32 = jnp.int32
I16 = jnp.int16
NN = (((1,), (0,)), ((), ()))
NT = (((1,), (1,)), ((), ()))
TN = (((0,), (0,)), ((), ()))

GH = 128
CAP = 4
SLOTS = 16
BACK = 3 * CAP
VMEM_LIMIT = 28 << 20
FINAL_PARTS = 2


def dot(left, right, dims=NN):
    return lax.dot_general(left, right, dims, preferred_element_type=F32)


def iota(shape, dim, dtype=I32):
    return lax.broadcasted_iota(I32, shape, dim).astype(dtype)


def hot(mask):
    return jnp.where(mask, 1.0, 0.0).astype(BF)


def column(row):
    return jnp.broadcast_to(row.astype(F32), (128, 128)).T


def half_silu(half):
    return half * (1.0 + jnp.tanh(half))


def rows_hot(index_row, count):
    table = lax.broadcasted_iota(I16, (count, index_row.shape[1]), 0)
    return jnp.where(table == index_row.astype(I16), BF(1), BF(0))


def over_back(row):
    return (row * (65536 // BACK + 1)) >> 16


def edge_halves(source_t, target_t, from_hot, to_hot):
    table = jnp.concatenate([source_t, target_t], axis=1)
    return dot(table, jnp.concatenate([from_hot, to_hot], axis=0)), to_hot


def edge_sum(half, to_hot):
    return dot(half_silu(half).astype(BF), to_hot, NT).astype(BF)


def edge_sums(first, last, halves, sums):
    ahead = halves(first)
    for b in range(first, last):
        now, ahead = ahead, halves(b + 1) if b + 1 < last else None
        sums[:, b * GH : (b + 1) * GH] = edge_sum(*now)


def layer_weights(w):
    first = jnp.concatenate([w[0].astype(F32).T, w[1].astype(F32).T], axis=0) * 0.5
    both = jnp.concatenate([w[3].astype(F32).T, dot(w[2], w[4]).T], axis=1) * 0.5
    last = w[5].astype(F32)
    last = last - jnp.mean(last, axis=1, keepdims=True)
    return first.astype(BF), both.astype(BF), last.T.astype(BF)


def node_updates(pieces, both, last):
    halves = [dot(both, jnp.concatenate(piece, axis=0)) for piece in pieces]
    centred = [dot(last, half_silu(half).astype(BF)) for half in halves]
    new = []
    for (rows_t, _), piece in zip(pieces, centred):
        spread = jnp.mean(piece * piece, axis=0, keepdims=True)
        new.append((rows_t.astype(F32) + piece * lax.rsqrt(spread + 1e-5)).astype(BF))
    return new


def local_edges(b, row_count, src, dst, valid, width):
    at = pl.ds(b * width, width)
    edge = src[:, at]
    line = jnp.where(
        edge < row_count, edge + GH, jnp.where(edge < row_count + GH, edge - row_count, edge)
    )
    to_row = jnp.where(valid[:, at] != 0, dst[:, at] - b * GH, -1)
    return rows_hot(line - b * GH, 3 * GH), rows_hot(to_row, GH)


def wanted_rows(place, lists):
    odd = place[1] % 2 == 1
    to_lower, to_upper = lists[0:1, :], lists[1:2, :]
    return jnp.concatenate(
        [jnp.where(odd, to_lower, to_upper), jnp.where(odd, to_upper, to_lower)], axis=1
    )


def inner_kernel(layer, rows_t, weights, src, dst, valid, out, first, both, last, ends, sums):
    row_count = rows_t.shape[1]
    blocks = row_count // GH
    width = src.shape[1] // blocks
    first[...], both[...], last[...] = layer_weights([weights[layer, i] for i in range(6)])
    ends[...] = dot(first[...], rows_t[...]).astype(BF)

    def halves(b):
        return edge_halves(
            ends[0:128, (b - 1) * GH : (b + 2) * GH],
            ends[128:256, b * GH : (b + 1) * GH],
            *local_edges(b, row_count, src, dst, valid, width),
        )

    edge_sums(1, blocks - 1, halves, sums)
    step = (row_count - 2 * GH) // 2
    ranges = [slice(start, start + step) for start in (GH, GH + step)]
    pieces = [(rows_t[:, at], sums[:, at]) for at in ranges]
    for at, new in zip(ranges, node_updates(pieces, both[...], last[...])):
        out[:, at] = new


def inner_pick_kernel(layer, place, lists, rows_t, weights, src, dst, valid, out, *refs):
    first, both, last, picked, ends, sums = refs
    inner_kernel(layer, rows_t, weights, src, dst, valid, out, first, both, last, ends, sums)
    count = out.shape[1]
    table = rows_hot(wanted_rows(place, lists) - GH, count - 2 * GH)
    picked[...] = dot(out[:, GH : count - GH], table).astype(BF)


def inner_pool_kernel(layer, cluster, rows_t, weights, src, dst, valid, out, *refs):
    first, both, last, pooled, ends, sums = refs
    inner_kernel(layer, rows_t, weights, src, dst, valid, out, first, both, last, ends, sums)
    count = out.shape[1]
    member = rows_hot(cluster[:, GH : count - GH], 128)
    pooled[...] = dot(out[:, GH : count - GH], member, NT)


def by_side(place, near, far):
    odd = place[1] % 2 == 1
    return jnp.where(odd, near, far), jnp.where(odd, far, near)


def ghost_rows(place, before, after):
    nothing = jnp.zeros_like(before)
    return jnp.where(place[2] == 0, nothing, before), jnp.where(place[3] == 0, nothing, after)


def end_blocks(place, rows_t, ghosts, first, both, last, src, dst, valid):
    row_count = rows_t.shape[1]
    blocks = row_count // GH
    width = src.shape[1] // blocks
    before, after = ghost_rows(place, *ghosts)
    head, tail = rows_t[:, 0 : 2 * GH], rows_t[:, row_count - 2 * GH :]
    line = jnp.concatenate([before, head, tail, after], axis=1)
    ends = dot(first[...], line).astype(BF)
    halves = [
        edge_halves(
            ends[0:128, at : at + 3 * GH],
            ends[128:256, at + own : at + own + GH],
            *local_edges(b, row_count, src, dst, valid, width),
        )
        for b, at, own in ((0, 0, GH), (blocks - 1, 3 * GH, GH))
    ]
    own = jnp.concatenate([head[:, :GH], tail[:, GH:]], axis=1)
    sums = jnp.concatenate([edge_sum(*half) for half in halves], axis=1)
    return node_updates([(own, sums)], both[...], last[...])[0]


def whole_layer(inner, new, out):
    count = out.shape[1]
    out[:, GH : count - GH] = inner[:, GH : count - GH]
    out[:, 0:GH] = new[:, :GH]
    out[:, count - GH :] = new[:, GH:]


def ends_pick_kernel(place, inner, *refs):
    lists, picked, slots, facts, out, near, far = refs[-7:]
    ghosts = [rows.T for rows in by_side(place, refs[1][...], refs[2][...])]
    new = end_blocks(place, refs[0], ghosts, *refs[3:-7])
    wanted = wanted_rows(place, lists)
    table = [rows_hot(wanted, GH), rows_hot(wanted - (out.shape[1] - GH), GH)]
    rows = picked[...].astype(F32) + dot(new, jnp.concatenate(table, axis=0))
    whole_layer(inner, new, out)
    for side, ref in enumerate((near, far)):
        ref[0:128, :] = rows[:, side * GH : (side + 1) * GH].astype(BF)
        ref[128:144, :] = slots[:, side * GH : (side + 1) * GH]
        ref[144:208, :] = facts[0:64, :]


def ends_pool_kernel(place, inner, *refs):
    cluster, pooled, slot_pick, facts, out, parcel, packed, sems = refs[-8:]
    ghosts = by_side(place, refs[2][0:128, :], refs[1][0:128, :])
    new = end_blocks(place, refs[0], ghosts, *refs[3:-8])
    count = out.shape[1]
    named = jnp.concatenate([cluster[:, 0:GH], cluster[:, count - GH :]], axis=1)
    partial = (pooled[...] + dot(new, rows_hot(named, 128), NT)).T.astype(BF)
    ids = by_side(place, refs[2][144:208, :], refs[1][144:208, :])
    lane = iota(ids[0].shape, 1)
    moved = [pltpu.roll(ids[side].astype(F32), CAP * (3 + side), 1) for side in (0, 1)]
    moved = [jnp.where(lane // CAP == 3 + side, moved[side], 0.0) for side in (0, 1)]
    added = moved[0] + moved[1]
    known = jnp.concatenate([added, jnp.zeros_like(added)], axis=0) + facts[...].astype(F32)
    sent = jnp.concatenate([partial, known.astype(BF)], axis=0)
    step = packed.shape[0] // 2
    copies = []
    for half in range(2):
        at = pl.ds(half * step, step)
        packed[at, :] = dot(slot_pick[at, :], sent).astype(BF)
        copies.append(pltpu.make_async_copy(packed.at[at, :], parcel.at[at, :], sems.at[half]))
        copies[-1].start()
    whole_layer(inner, new, out)
    for copy in copies:
        copy.wait()


def turn_kernel(nodes, rows_t):
    rows_t[...] = nodes[...].T


def pick_kernel(place, rows_t, lists, near, far, meta_pick, spread):
    picked = dot(rows_t[...], rows_hot(wanted_rows(place, lists), rows_t.shape[1])).astype(BF)
    near[...], far[...] = picked[:, :GH], picked[:, GH:]
    count, total = meta_pick.shape
    owners = count // 3
    wide, pick = iota((count, total), 1), iota((count, total), 0)
    meta_pick[...] = hot(wide == SLOTS * (pick % owners) + 3 * CAP + pick // owners)
    spread[...] = hot((wide // SLOTS == pick % owners) & (wide % SLOTS // CAP == pick // owners))


def prepare_kernel(
    place, lists, cluster, owner, coarse_row, ghosts, slot_pick, facts, slot_of, slots
):
    member = rows_hot(cluster[...], 128)
    counts = jnp.sum(member.astype(F32), axis=1, keepdims=True)
    owner_row = owner[...].astype(F32)
    by_row, by_lane = column(owner_row), jnp.broadcast_to(owner_row, (128, 128))
    sub, lane = iota((128, 128), 0), iota((128, 128), 1)
    same = by_row == by_lane
    place_col = jnp.sum(jnp.where(same & (lane < sub), 1.0, 0.0), axis=1, keepdims=True)
    place_row = jnp.sum(jnp.where(same & (sub < lane), 1.0, 0.0), axis=0, keepdims=True)
    slot_row = owner_row * CAP + place_row
    owners = slot_pick.shape[0] // SLOTS
    every = dot(jnp.broadcast_to(slot_row, (16, 128)).astype(BF), member).astype(BF)
    slots[...] = dot(every, rows_hot(wanted_rows(place, lists), cluster.shape[1])).astype(BF)
    row = iota((owners * SLOTS, 128), 0)
    to, at = row // SLOTS, row % SLOTS
    label = jnp.where(
        at < CAP,
        CAP * to + at,
        jnp.where(
            at < 2 * CAP,
            CAP * (to - 1) + at - CAP,
            jnp.where(at < 3 * CAP, CAP * (to + 1) + at - 2 * CAP, -1),
        ),
    )
    slot_pick[:, 0:128] = hot(label.astype(F32) == slot_row)
    back_row = iota(slot_of.shape, 0)
    back_to = over_back(back_row)
    back_at = back_row - BACK * back_to
    slot_of[...] = hot(
        jnp.where(back_at < CAP, CAP * back_to + back_at, -1).astype(F32) == slot_row
    )
    fact = jnp.where(
        at == 3 * CAP,
        to,
        jnp.where(
            at == 3 * CAP + 1,
            to - 1,
            jnp.where(at == 3 * CAP + 2, to + 1, jnp.where(at == 3 * CAP + 3, 127, -1)),
        ),
    )
    slot_pick[:, 128:256] = hot(fact == iota(fact.shape, 1))
    high = jnp.floor(counts / 16.0)
    low = counts - 16.0 * high
    lanes = lane.astype(F32)
    values = (
        jnp.where(lanes == place_col, column(coarse_row[...]), 0.0)
        + jnp.where(lanes == place_col + CAP, high, 0.0)
        + jnp.where(lanes == place_col + 2 * CAP, low, 0.0)
    ).astype(BF)
    meta = dot(hot(by_lane == sub.astype(F32)), values)
    each = ghosts.shape[2]
    listed = jnp.concatenate(
        [ghosts[0, 0:1], ghosts[0, 1:2], jnp.zeros((1, 128 - 2 * each), I32)], axis=1
    ).astype(F32)
    facts[...] = jnp.where(sub == 127, listed, meta).astype(BF)


def received_kernel(place, got, meta_pick, spread, part, own_metas):
    total = got.shape[0]
    owners = total // SLOTS
    here = place[0]
    metas = dot(meta_pick[...], got[...]).astype(BF)
    own_metas[...] = metas[0:owners]
    facts = dot(metas, spread[...], TN)[0:16]
    lane = iota((1, total), 1)
    turn = iota((16, total), 0) - iota((16, total), 1) % CAP

    def fact(number):
        return jnp.sum(jnp.where(turn == CAP * number, facts, 0.0), axis=0, keepdims=True)

    group = lane % SLOTS // CAP
    key = jnp.where(group < 3, fact(0) + (128 * group).astype(F32), -1.0)
    below = got[pl.ds(pl.multiple_of(jnp.maximum(here - 1, 0) * SLOTS, SLOTS), SLOTS), :]
    above = got[pl.ds(pl.multiple_of(jnp.minimum(here + 1, owners - 1) * SLOTS, SLOTS), SLOTS), :]
    below = column(below.astype(F32)[SLOTS - 1 : SLOTS, :])[16:32]
    above = column(above.astype(F32)[SLOTS - 1 : SLOTS, :])[0:16]
    label = jnp.concatenate(
        [
            iota((128, 128), 0, F32),
            jnp.where(here > 0, below + 128.0, -7.0),
            jnp.where(here < owners - 1, above + 256.0, -7.0),
            jnp.full((96, 128), -7.0, F32),
        ],
        axis=0,
    )
    label = jnp.concatenate([label] * (total // 128), axis=1)
    table = hot(label == key)
    part[0:160, :] = dot(table[0:160], got[...]).astype(BF)
    counted = dot(
        jnp.concatenate([fact(1), fact(2), jnp.zeros((6, total), F32)], axis=0).astype(BF),
        table,
        NT,
    )
    count = counted[0:1] * 16.0 + counted[1:2]
    third = jnp.floor(count / 65536.0)
    second = jnp.floor((count - 65536.0 * third) / 256.0)
    first = count - 65536.0 * third - 256.0 * second
    digits = [first, second, third]
    part[160:176, :] = jnp.concatenate(
        [d[:, 0:128] for d in digits]
        + [d[:, 128:256] for d in digits]
        + [jnp.zeros((10, 128), F32)],
        axis=0,
    ).astype(BF)


def ready_kernel(own_metas, weights, src, dst, near, far, *outs):
    back, first, both, last, from_hot, to_hot, first3, both3, last3 = outs
    owners = own_metas.shape[0]
    total = BACK * owners
    ids = dot(hot(over_back(iota((total, owners), 0)) == iota((total, owners), 1)), own_metas[...])
    row = iota((total, 128), 0)
    at = row - BACK * over_back(row)
    lanes = iota((total, 128), 1)
    wanted = jnp.where(at < CAP, at, at + 2 * CAP)
    named = jnp.sum(jnp.where(lanes == wanted, ids, 0.0), axis=1, keepdims=True)
    back[...] = hot(lanes.astype(F32) == named)
    first[...], both[...], last[...] = layer_weights([weights[2, i] for i in range(6)])
    first3[...], both3[...], last3[...] = layer_weights([weights[3, i] for i in range(6)])
    from_hot[...] = rows_hot(src[...], 160)
    to_hot[...] = rows_hot(dst[...], 128)


def coarse_kernel(own, other1, other2, other3, back, first, both, last, from_hot, to_hot, out, reply):
    whole = (own[...].astype(F32) + other1[...].astype(F32)) + (
        other2[...].astype(F32) + other3[...].astype(F32)
    )

    def counts(at):
        row = whole[at : at + 1] + 256.0 * whole[at + 1 : at + 2] + 65536.0 * whole[at + 2 : at + 3]
        return jnp.maximum(row, 1.0)

    rows_t = (whole[0:128].T / counts(160)).astype(BF)
    ghosts = jnp.concatenate([whole[128:160], jnp.zeros((96, 128), F32)], axis=0)
    ghosts_t = (ghosts.T / counts(163)).astype(BF)
    ends = dot(first[...], jnp.concatenate([rows_t, ghosts_t], axis=1)).astype(BF)
    half = dot(ends[0:128, 0:160], from_hot[...]) + dot(ends[128:256, 0:128], to_hot[...])
    sums = dot(half_silu(half).astype(BF), to_hot[...], NT).astype(BF)
    new = node_updates([(rows_t, sums)], both[...], last[...])[0].T
    out[...] = new
    reply[...] = dot(back[...], new).astype(BF)


def final_kernel(
    place,
    rows_t,
    reply,
    slot_of,
    cluster,
    early_far,
    early_near,
    from_far,
    from_near,
    first,
    both,
    last,
    src,
    dst,
    valid,
    out,
    line,
    ends,
    sums,
    done,
    sems,
):
    row_count = rows_t.shape[1]
    blocks = row_count // GH
    width = src.shape[1] // blocks
    tables = [slot_of[...]]
    for at, slots in enumerate(by_side(place, early_near[128:144, :], early_far[128:144, :])):
        slot = slots.astype(F32).astype(I32)[0:1]
        tables.append(rows_hot(slot // CAP * BACK + slot % CAP + CAP * (at + 1), reply.shape[0]))
    coarse = dot(reply[...], jnp.concatenate(tables, axis=1), TN)
    member = rows_hot(cluster[...], 128)
    before, after = by_side(place, from_near[...], from_far[...])
    before = (before.astype(F32) + coarse[:, 128:256]).astype(BF)
    after = (after.astype(F32) + coarse[:, 256:384]).astype(BF)
    line[:, 0:GH], line[:, GH + row_count :] = ghost_rows(place, before, after)
    line[:, GH : GH + row_count] = (
        rows_t[...].astype(F32) + dot(coarse[:, 0:128].astype(BF), member)
    ).astype(BF)
    ends[...] = dot(first[...], line[...]).astype(BF)
    parts = sems.shape[0]
    step = row_count // parts
    copies = []

    def halves(b):
        return edge_halves(
            ends[0:128, b * GH : (b + 3) * GH],
            ends[128:256, (b + 1) * GH : (b + 2) * GH],
            *local_edges(b, row_count, src, dst, valid, width),
        )

    edge_sums(0, blocks, halves, sums)
    starts = [part * step for part in range(parts)]
    pieces = [
        (line[:, GH + start : GH + start + step], sums[:, start : start + step]) for start in starts
    ]
    for part, new in enumerate(node_updates(pieces, both[...], last[...])):
        start = starts[part]
        at = pl.ds(start, step)
        done[at, :] = new.T
        copies.append(pltpu.make_async_copy(done.at[at, :], out.at[at, :], sems.at[part]))
        copies[-1].start()
    for copy in copies:
        copy.wait()


def run(kernel, outs, args, scalars=0, layer=None, scratch=(), flops=0, out_space=pltpu.VMEM, wide=None, loose=None, name=None):
    specs = []
    for i in range(len(args)):
        specs.append(pl.BlockSpec(memory_space=pltpu.SMEM if i < scalars else pltpu.VMEM))
    return pl.pallas_call(
        kernel if layer is None else functools.partial(kernel, layer),
        out_shape=[
            jax.ShapeDtypeStruct(shape, F32 if i == wide else BF) for i, shape in enumerate(outs)
        ],
        in_specs=specs,
        out_specs=[
            pl.BlockSpec(memory_space=pl.ANY if i == loose else out_space) for i in range(len(outs))
        ],
        scratch_shapes=scratch,
        compiler_params=pltpu.CompilerParams(vmem_limit_bytes=VMEM_LIMIT),
        cost_estimate=pl.CostEstimate(flops=flops, bytes_accessed=1 << 20, transcendentals=0),
        name=name,
    )(*args)


def on_device(
    nodes,
    weights,
    edge_src,
    edge_dst,
    edge_valid,
    ghost_list,
    cluster_of,
    owner,
    coarse_row,
    coarse_src,
    coarse_dst,
    coarse_ghosts,
):
    count, width = nodes.shape
    doms, subs = lax.axis_size("dom"), lax.axis_size("sub")
    dom, sub = lax.axis_index("dom"), lax.axis_index("sub")
    chain = doms * subs
    index = dom * subs + sub
    place = jnp.stack([dom, sub, index, chain - 1 - index]).astype(I32)
    lists = ghost_list[0]
    edges = (edge_src, edge_dst, edge_valid)
    ghost = (width, GH)
    rows_t = (width, count)
    forms = [(2 * width, width), (width, 2 * width), (width, width)]
    near_pairs = [(i, i ^ 1) for i in range(chain)]
    far_pairs = [(i, (i + 1 if i % 2 else i - 1) % chain) for i in range(chain)]

    def swap(near, far):
        from_far = lax.ppermute(far, ("dom", "sub"), far_pairs)
        from_near = lax.ppermute(near, ("dom", "sub"), near_pairs)
        return from_far, from_near

    def inner(kernel, before, states, layer, more, **options):
        out, first, both, last, extra = run(
            kernel,
            [rows_t] + forms + [more],
            before + (states, weights) + edges,
            layer=layer,
            scratch=[pltpu.VMEM((2 * width, count), BF), pltpu.VMEM(rows_t, BF)],
            flops=4 * 10**9,
            **options,
        )
        return out, (first, both, last), extra

    wanted = lists.reshape(-1, 1) == jnp.arange(count, dtype=I32)[None, :]
    picked = dot(wanted.astype(BF), nodes).astype(BF)
    odd = sub % 2 == 1
    ghosts = swap(
        jnp.where(odd, picked[:GH], picked[GH:]), jnp.where(odd, picked[GH:], picked[:GH])
    )
    (states,) = run(turn_kernel, [rows_t], (nodes,), flops=3 * 10**8, name="turn")
    slot_pick, facts, slot_of, slots = run(
        prepare_kernel,
        [(doms * SLOTS, 256), (128, 128), (doms * BACK, 128), (16, 2 * GH)],
        (place, lists, cluster_of, owner.reshape(1, -1), coarse_row, coarse_ghosts),
        scalars=1,
        flops=10**9,
        name="prepare",
    )
    middle, now, picked = inner(
        inner_pick_kernel, (place, lists), states, 0, (width, 2 * GH), scalars=1, name="inner_pick"
    )
    early = (GH + 16 + doms, GH)
    states, near, far = run(
        ends_pick_kernel,
        [rows_t, early, early],
        (place, middle, states) + ghosts[::-1] + now + edges + (lists, picked, slots, facts),
        scalars=1,
        flops=10**9,
        name="ends_pick",
    )
    early = swap(near, far)
    middle, now, pooled = inner(
        inner_pool_kernel, (cluster_of,), states, 1, (width, 128), wide=4, name="inner_pool"
    )
    states, parcel = run(
        ends_pool_kernel,
        [rows_t, (doms * SLOTS, width)],
        (place, middle, states) + early + now + edges + (cluster_of, pooled, slot_pick, facts),
        scalars=1,
        scratch=[pltpu.VMEM((doms * SLOTS, width), BF), pltpu.SemaphoreType.DMA((2,))],
        loose=1,
        flops=10**9,
        name="ends_pool",
    )
    near, far, meta_pick, spread = run(
        pick_kernel,
        [ghost, ghost] + [(3 * doms, doms * SLOTS)] * 2,
        (place, states, lists),
        scalars=1,
        flops=10**9,
        name="pick",
    )
    ghosts = swap(near, far)

    def exchange(rows):
        shape = rows.shape
        each = 4 if shape[0] // doms % 8 else 8
        rows = rows.reshape(-1, each, width)
        rows = lax.all_to_all(rows, "dom", split_axis=0, concat_axis=0, tiled=True)
        return rows.reshape(shape)

    part, own_metas = run(
        received_kernel,
        [(176, width), (doms, width)],
        (place, exchange(parcel), meta_pick, spread),
        scalars=1,
        flops=10**9,
        name="received",
    )
    others = [lax.ppermute(part, "sub", [(i, i ^ k) for i in range(subs)]) for k in (1, 2, 3)]
    back, *ready = run(
        ready_kernel,
        [(doms * BACK, width)]
        + forms
        + [(160, coarse_src.shape[1]), (128, coarse_src.shape[1])]
        + forms,
        (own_metas, weights, coarse_src, coarse_dst) + ghosts,
        flops=10**9,
        name="ready",
    )
    coarse, reply = run(
        coarse_kernel,
        [(128, width), (doms * BACK, width)],
        (part, *others, back, *ready[:5]),
        flops=10**9,
        name="coarse",
    )
    (last,) = run(
        final_kernel,
        [nodes.shape],
        (place, states, exchange(reply), slot_of, cluster_of) + early + ghosts + tuple(ready[5:8]) + edges,
        scalars=1,
        scratch=[
            pltpu.VMEM((width, count + 2 * GH), BF),
            pltpu.VMEM((2 * width, count + 2 * GH), BF),
            pltpu.VMEM(rows_t, BF),
            pltpu.VMEM(nodes.shape, BF),
            pltpu.SemaphoreType.DMA((FINAL_PARTS,)),
        ],
        out_space=pl.ANY,
        flops=5 * 10**9,
        name="final",
    )
    return (last, coarse)


def solution(mesh):
    placed = (
        P(("dom", "sub"), None),
        P(),
        P(("dom", "sub"), None),
        P(("dom", "sub"), None),
        P(("dom", "sub"), None),
        P(("dom", "sub"), None, None),
        P(("dom", "sub"), None),
        P(("dom", "sub"), None, None),
        P(("dom", "sub"), None),
        P("dom", None),
        P("dom", None),
        P("dom", None, None),
    )
    return jax.shard_map(
        on_device,
        mesh=mesh,
        in_specs=placed,
        out_specs=(P(("dom", "sub"), None), P("dom", None)),
        check_vma=False,
    )
```
